512 devices in a mesh: lat: 8 (over z), lon: 16 (over y_lo, x, core), obs: 4 (over y_hi).
Axes of the slice: x: 4, y: 8 (y_hi: 4, y_lo: 2; y = y_hi * 2 + y_lo), z: 8, core: 2. Of those that a mesh axis runs over, the one named last changes fastest.
Arguments:
- control: float32 [4, 25, 64, 2048], P('obs', None, 'lat', 'lon'), may hold values from -6 to 6
- residual: float32 [4, 25, 64, 2048], P('obs', None, 'lat', 'lon'), may hold values from -6 to 6
- direction: float32 [4, 25, 64, 2048], P('obs', None, 'lat', 'lon'), may hold values from -6 to 6
- land_mask: int32 [64, 2048], P('lat', 'lon'), may hold values 0 or 1
- kappa_east: float32 [64, 2048], P('lat', 'lon'), may hold values from 0.25 to 4
- kappa_north: float32 [64, 2048], P('lat', 'lon'), may hold values from 0.25 to 4
- sigma: float32 [4, 64, 2048], P('obs', 'lat', 'lon'), may hold values from 0.5 to 2
- obs_weight: float32 [4, 25, 32768], P('obs', None, ('lat', 'lon')), may hold values from -6 to 6
- obs_cell: int32 [32768], P(('lat', 'lon')), may hold values from 0 to 1023
- obs_owner: int32 [32768, 1], P(('lat', 'lon')), may hold values from 0 to 127; in each aligned block of 256 rows (0 to 255, 256 to 511, ...) at most 4 rows name the same one
- error_inverse: float32 [128, 25, 25], P(('lat', 'lon')), may hold values from -1 to 2, as said below
Outputs:
- control_next: float32 [4, 25, 64, 2048], P('obs', None, 'lat', 'lon')
- residual_next: float32 [4, 25, 64, 2048], P('obs', None, 'lat', 'lon')
- direction_next: float32 [4, 25, 64, 2048], P('obs', None, 'lat', 'lon')
The draws below stay inside these ranges and needn't reach their ends.
Inputs may be any that keep to these rules, and one draw needn't show every extreme that they name: `obs_owner`: in the rows of one device no owner is named by more than 4 rows. `error_inverse`: each matrix is symmetric with positive diagonal exceeding the sum of magnitudes of its row's other entries.
All inputs are finite; a program needn't handle non-finite values. No bound on the sum of `land_mask` on one device may be relied on, other than what follows from the above.
Results may differ from the reference program's by a relative error of at most 0.000078.
Values sent between devices are 32-bit elements; how exact they have to be, the bound alone decides.
No kernel may reach another device: no remote copies, remote signals or barrier semaphores. Data moves between devices by JAX's collectives and lax.ppermute only.
A program may use at most 64 MiB of HBM per device.

```python
import math
import jax
import jax.numpy as jnp
import numpy as np
from jax import lax

FIELDS = 4
LEV = 25
CY = 8
CX = 128
SLOTS = 256
SWEEPS = 4
NY = 64
NX = 2048
OWNERS = 128
SLOTTOT = 32768
CAP = 4
N_LON = 16


def draw_error_inverse(key, part):
    key = jax.random.fold_in(key, 7)
    first, second = jax.random.split(key)
    offdiag = jax.random.uniform(first, (OWNERS, LEV, LEV), jnp.float32, -0.8 / LEV, 0.8 / LEV)
    offdiag = 0.5 * (offdiag + jnp.swapaxes(offdiag, 1, 2))
    diagonal = jnp.exp(jax.random.uniform(second, (OWNERS, LEV), jnp.float32, 0.0, 0.6931))
    unit = jnp.eye(LEV, dtype=jnp.float32)
    return offdiag * (1.0 - unit) + unit * diagonal[:, :, None]


def plant(result, own_key, smallest, top_value):
    longest = result.shape.index(max(result.shape))
    spots = []
    for shift in (0, 1):
        where = [jax.random.randint(jax.random.fold_in(own_key, axis), (), 0, length) for axis, length in enumerate(result.shape)]
        where[longest] = (where[longest] + shift) % result.shape[longest]
        spots.append(tuple(where))
    return result.at[spots[0]].set(smallest).at[spots[1]].set(top_value)


def level_of(own_key, dims, cuts, low, high):
    factor_of, own = 1.0, jax.random.fold_in(own_key, 6)
    for dim, shards_of in cuts:
        draws = jnp.exp(jax.random.uniform(jax.random.fold_in(own, dim), (shards_of,), jnp.float32, low / len(cuts), high / len(cuts)))
        factor_of = factor_of * jnp.repeat(draws, dims[dim] // shards_of).reshape([-1 if axis == dim else 1 for axis in range(len(dims))])
    return factor_of


def routed_block(own_key, own, number, rows, number_of, top, reach, slope):
    order = jax.random.permutation(own_key, number_of)
    heavy_load, common = load_shares(number_of, rows * top, reach, slope, True), load_shares(number_of, rows * top, reach, slope, False)
    places = jnp.arange(number_of)

    def named(lengths, turn):
        used = int((lengths > 0).sum())
        fixed = max(1, used // 4)
        moved = fixed + (places - fixed + turn * (used - fixed)) % max(1, number_of - fixed)
        return jnp.zeros((number_of,), jnp.int32).at[order[jnp.where(places < fixed, places, moved)]].set(jnp.asarray(lengths, jnp.int32))

    lengths = jnp.where(number % 4 == 0, named(heavy_load, number // 4), named(common, number - number // 4 - 1))
    mixed = jax.random.permutation(jax.random.fold_in(own, 3), number_of)
    source_of, taker = mixed[0:number_of // 2 * 2:2], mixed[1:number_of // 2 * 2:2]
    margin = jnp.minimum(lengths[source_of] - 1, reach - lengths[taker]) // 2
    margin = jnp.where((source_of == order[0]) | (taker == order[0]) | (lengths[taker] == 0), 0, jnp.maximum(margin, 0))
    moved = jax.random.randint(jax.random.fold_in(own, 4), (number_of // 2,), 0, 1 << 20) % (margin + 1)
    lengths = lengths.at[source_of].add(-moved).at[taker].add(moved)
    items = jnp.searchsorted(jnp.cumsum(lengths), jnp.arange(rows * top), side="right").astype(jnp.int32)
    table = items.reshape(top, rows).T
    table = table[jax.random.permutation(jax.random.fold_in(own, 1), rows)]
    turn = jax.random.randint(jax.random.fold_in(own, 2), (rows, 1), 0, top)
    return jnp.take_along_axis(table, (jnp.arange(top)[None, :] + turn) % top, axis=1)


def load_shares(count, total, bound, skew, full):
    loads = [(1 << 20) // math.isqrt(grade ** skew) + 1 for grade in range(1, count + 1)]
    largest = bound if full else min(bound, max(-(-total // count), total * loads[0] // sum(loads)))
    least = 1 if total - largest >= count - 1 else 0
    given, surplus = [largest] + [least] * (count - 1), total - largest - least * (count - 1)
    while surplus > 0:
        movable = [i for i in range(1, count) if given[i] < largest] or [i for i in range(1, count) if given[i] < bound]
        pool, budget = sum([loads[i] for i in movable]), surplus
        for i in movable:
            more = min(bound - given[i], max(1, budget * loads[i] // pool), surplus)
            given[i] = given[i] + more
            surplus = surplus - more
    return np.array(given)


def gaussian(rng, dims, deviation, limit, pieces=(), held_as=jnp.bfloat16):
    entries = deviation * jax.random.normal(rng, dims, jnp.float32)
    if pieces:
        entries = entries * level_of(rng, dims, pieces, -0.22, 0.18)
    return jnp.clip(entries, -limit, limit).astype(held_as)


def setup_inputs(seed: int = 0) -> dict:
    key_of = jax.random.split(jax.random.key(seed), 12)
    control = gaussian(key_of[0], (FIELDS, LEV, NY, NX), 1.0, 6.0, ((0, 4), (2, 8), (3, 16)), jnp.float32)
    residual = gaussian(key_of[1], (FIELDS, LEV, NY, NX), 1.0, 6.0, ((0, 4), (2, 8), (3, 16)), jnp.float32)
    direction = gaussian(key_of[2], (FIELDS, LEV, NY, NX), 1.0, 6.0, ((0, 4), (2, 8), (3, 16)), jnp.float32)
    land_mask = plant((jax.random.randint(key_of[3], (NY, NX), 0, 5) < 4).astype(jnp.int32), jax.random.fold_in(key_of[3], 1), 0, 1)
    kappa_east = jnp.clip(jnp.exp(math.log(4.0) - 2.7725887 * jax.random.uniform(key_of[4], (NY, NX), jnp.float32) ** level_of(key_of[4], (NY, NX), ((0, 8), (1, 16)), -0.2, 0.2)), 0.25, 4.0)
    kappa_north = jnp.clip(jnp.exp(math.log(4.0) - 2.7725887 * jax.random.uniform(key_of[5], (NY, NX), jnp.float32) ** level_of(key_of[5], (NY, NX), ((0, 8), (1, 16)), -0.2, 0.2)), 0.25, 4.0)
    sigma = jnp.clip(jnp.exp(math.log(2.0) - 1.3862944 * jax.random.uniform(key_of[6], (FIELDS, NY, NX), jnp.float32) ** level_of(key_of[6], (FIELDS, NY, NX), ((0, 4), (1, 8), (2, 16)), -0.2, 0.2)), 0.5, 2.0)
    obs_weight = gaussian(key_of[7], (FIELDS, LEV, SLOTTOT), 1.0, 6.0, ((0, 4), (2, 128)), jnp.float32)
    obs_cell = plant(jax.random.randint(key_of[8], (SLOTTOT,), 0, CY * CX), jax.random.fold_in(key_of[8], 1), 0, (CY * CX) - 1).astype(jnp.int32)
    obs_owner_keys = jax.random.split(jax.random.fold_in(key_of[9], 1), SLOTTOT // SLOTS)
    obs_owner_turns = jax.random.permutation(jax.random.fold_in(key_of[9], 3), SLOTTOT // SLOTS)
    obs_owner = jax.vmap(lambda own, number: routed_block(jax.random.fold_in(key_of[9], 2), own, number, SLOTS, OWNERS, 1, CAP, 2))(obs_owner_keys, obs_owner_turns).reshape((SLOTTOT, 1))
    error_inverse = draw_error_inverse(jax.random.fold_in(key_of[11], 71), 0)
    return {"control": control, "residual": residual, "direction": direction, "land_mask": land_mask, "kappa_east": kappa_east, "kappa_north": kappa_north, "sigma": sigma, "obs_weight": obs_weight, "obs_cell": obs_cell, "obs_owner": obs_owner, "error_inverse": error_inverse}


def extend(field):
    wrapped = jnp.concatenate([field[..., -1:], field, field[..., :1]], axis=-1)
    widths = [(0, 0)] * (field.ndim - 2) + [(1, 1), (0, 0)]
    return jnp.pad(wrapped, widths)


def face_terms(land_mask, kappa_east, kappa_north):
    flags = extend(land_mask.astype(jnp.float32))
    east = extend(kappa_east)
    north = extend(kappa_north)
    east_face = east[:, :-1] * flags[:, :-1] * flags[:, 1:]
    north_face = north[:-1] * flags[:-1] * flags[1:]
    return east_face[1:-1, 1:], east_face[1:-1, :-1], north_face[1:, 1:-1], north_face[:-1, 1:-1]


def diffuse(source, terms):
    c_east, c_west, c_north, c_south = terms
    scale = 1.0 + c_east + c_west + c_north + c_south
    iterate = jnp.zeros_like(source)
    for sweep in range(SWEEPS):
        padded = extend(iterate)
        near = c_east * padded[:, 1:-1, 2:] + c_west * padded[:, 1:-1, :-2] + c_north * padded[:, 2:, 1:-1] + c_south * padded[:, :-2, 1:-1]
        iterate = (source + near) / scale
    return iterate


def reference(control, residual, direction, land_mask, kappa_east, kappa_north, sigma, obs_weight, obs_cell, obs_owner, error_inverse):
    terms = face_terms(land_mask, kappa_east, kappa_north)
    spread = (sigma * land_mask.astype(jnp.float32)[None])[:, None]
    flat_shape = (FIELDS * LEV, NY, NX)
    state = spread * diffuse(direction.reshape(flat_shape), terms).reshape(direction.shape)
    device = jnp.arange(SLOTTOT, dtype=jnp.int32) // SLOTS
    rows = (device // N_LON) * CY + obs_cell // CX
    cols = (device % N_LON) * CX + obs_cell % CX
    picked = state[:, :, rows, cols]
    column = jnp.sum(obs_weight * picked, axis=0)
    tables = error_inverse[obs_owner[:, 0]]
    weighted = jnp.einsum("klm,mk->lk", tables, column, precision=lax.Precision.HIGHEST)
    adjoint = jnp.zeros(direction.shape, jnp.float32).at[:, :, rows, cols].add(obs_weight * weighted[None])
    image = direction + diffuse((spread * adjoint).reshape(flat_shape), terms).reshape(direction.shape)
    norm_now = jnp.sum(residual * residual)
    alpha = norm_now / jnp.sum(direction * image)
    control_next = control + alpha * direction
    residual_next = residual - alpha * image
    norm_next = jnp.sum(residual_next * residual_next)
    direction_next = residual_next + (norm_next / norm_now) * direction
    return control_next, residual_next, direction_next
```

```python
import functools

import jax
import jax.numpy as jnp
from jax import lax
from jax.experimental import pallas as pl
from jax.experimental.pallas import tpu as pltpu
from jax.sharding import PartitionSpec as P

LEV = 25
PADLEV = 32
ROWS = 8
COLS = 128
SLOTS = 256
SHIFT = 4
SWEEPS = 4
GROUP = 5

M_FLAG, M_EAST, M_NORTH, M_SIGMA, M_WEIGHT, M_PLACE, M_TILES = 25, 26, 27, 28, 29, 37, 38
LIMIT = 48 * 1024 * 1024


def shifted(x, by, axis):
    return pltpu.roll(x, by % x.shape[axis], axis)


def split(x, parts):
    out = []
    for _ in range(parts):
        part = x.astype(jnp.bfloat16)
        out.append(part)
        x = x - part.astype(jnp.float32)
    return out


def frame(refs, tile):
    low = jnp.concatenate([refs[0][tile], refs[1][tile]], axis=-1)
    high = jnp.concatenate([refs[2][tile], refs[3][tile]], axis=-1)
    return jnp.concatenate([low, high], axis=-2)


def scaled_faces(ke, kn):
    kw = shifted(ke, 1, 1)
    ks = shifted(kn, 1, 0)
    inverse = 1.0 / (1.0 + ke + kw + kn + ks)
    return inverse, ke * inverse, kw * inverse, kn * inverse, ks * inverse


def diffuse(source, scaled):
    inverse, ke, kw, kn, ks = [term[None] for term in scaled]
    scaled_source = source * inverse
    x = scaled_source
    for _ in range(SWEEPS - 1):
        x = (
            scaled_source
            + ke * shifted(x, -1, 2)
            + kw * shifted(x, 1, 2)
            + kn * shifted(x, -1, 1)
            + ks * shifted(x, 1, 1)
        )
    return x


def south_west(x):
    axis = x.ndim - 2
    x = shifted(shifted(x, SHIFT, axis + 1), SHIFT, axis)
    return x[..., ROWS:, COLS:]


def north_east(x):
    axis = x.ndim - 2
    x = shifted(shifted(x, -SHIFT, axis + 1), -SHIFT, axis)
    return x[..., :ROWS, :COLS]


def place_rows(refs, half):
    picked = []
    for west in (0, 1):
        ref = refs[2 * half + (1 - west)]
        cell = ref[M_PLACE, 0:2, :].astype(jnp.int32)
        row, col = cell // COLS, cell % COLS
        if half == 1:
            inside = row < ROWS - SHIFT
        else:
            inside = row >= SHIFT
            row = row - SHIFT
        if west:
            inside = inside & (col >= COLS - SHIFT)
            col = col - (COLS - SHIFT)
        else:
            inside = inside & (col < COLS - SHIFT)
            col = col + SHIFT
        place = jnp.where(inside, row * COLS + col, -1)
        picked += [place[0:1], place[1:2]]
    return jnp.concatenate(picked, axis=1)


def weights_of(refs, half):
    picked = []
    for west in (0, 1):
        ref = refs[2 * half + (1 - west)]
        for part in (0, 1):
            first = M_WEIGHT + 4 * part
            picked.append(ref[first : first + 4].reshape(PADLEV, COLS))
    return jnp.concatenate(picked, axis=1)


def owners_of(refs, half):
    picked = []
    for west in (0, 1):
        ref = refs[2 * half + (1 - west)]
        owner = ref[M_PLACE, 2:4, :].astype(jnp.int32)
        picked += [owner[0:1], owner[1:2]]
    return jnp.concatenate(picked, axis=1)


def one_hot(index, length):
    rows = lax.broadcasted_iota(jnp.int32, (length, index.shape[1]), 0)
    return jnp.where(rows == index, 1.0, 0.0).astype(jnp.bfloat16)


def pack_kernel(d, flag, east, north, sigma, weight, cell, owner, table, msg, tables, wide):
    msg[0:LEV] = d[...]
    msg[M_FLAG] = flag[...].astype(jnp.float32)
    msg[M_EAST] = east[...]
    msg[M_NORTH] = north[...]
    msg[M_SIGMA] = sigma[...]
    for part in (0, 1):
        first = M_WEIGHT + 4 * part
        columns = slice(part * COLS, (part + 1) * COLS)
        for i in range(3):
            msg[first + i] = weight[8 * i : 8 * i + 8, columns]
        msg[first + 3] = jnp.zeros((ROWS, COLS), jnp.float32)
        msg[first + 3, 0:1, :] = weight[24:25, columns]
    msg[M_PLACE] = jnp.zeros((ROWS, COLS), jnp.float32)
    msg[M_PLACE, 0:2, :] = cell[...].astype(jnp.float32)
    msg[M_PLACE, 2:4, :] = owner[...].astype(jnp.float32)
    wide[...] = jnp.zeros_like(wide)
    wide[0:LEV, 0:LEV] = table[...]
    tile = jnp.zeros((ROWS, COLS), jnp.float32)
    for q in range(4):
        tile = tile + shifted(wide[pl.ds(q, 8, stride=4), :], 32 * q, 1)
    tables[...] = jnp.broadcast_to(tile[None], tables.shape)


def pick_kernel(sw, s, w, o, part, aux, held):
    refs = (sw, s, w, o)
    flag = frame(refs, M_FLAG)
    ke = frame(refs, M_EAST) * flag * shifted(flag, -1, 1)
    kn = frame(refs, M_NORTH) * flag * shifted(flag, -1, 0)
    row = lax.broadcasted_iota(jnp.int32, kn.shape, 0)
    edge = (row == ROWS - 1) & (lax.axis_index("lat") == 0)
    kn = jnp.where(edge, 0.0, kn)
    spread = frame(refs, M_SIGMA) * flag
    aux[0] = south_west(spread)
    aux[1] = south_west(ke)
    aux[2] = south_west(kn)
    scaled = scaled_faces(ke, kn)
    spread_here = aux[0]
    held[LEV * ROWS :, :] = jnp.zeros((held.shape[0] - LEV * ROWS, COLS), jnp.float32)
    for g in range(LEV // GROUP):
        source = frame(refs, slice(g * GROUP, (g + 1) * GROUP))
        x = south_west(diffuse(source, scaled)) * spread_here[None]
        held[g * GROUP * ROWS : (g + 1) * GROUP * ROWS, :] = x.reshape(GROUP * ROWS, COLS)
    for half in (1, 0):
        first = SHIFT * half
        state = jnp.concatenate(
            [held[pl.ds(first + r, PADLEV, stride=ROWS), :] for r in range(SHIFT)], axis=1
        )
        hot = one_hot(place_rows(refs, half), SHIFT * COLS)
        stacked = jnp.concatenate(split(state, 3), axis=0)
        got = jnp.dot(stacked, hot, preferred_element_type=jnp.float32)
        got = got[0:PADLEV] + got[PADLEV : 2 * PADLEV] + got[2 * PADLEV :]
        got = got * weights_of(refs, half)
        for c in range(4):
            at = (4 * half + c) * LEV
            part[at : at + LEV, :] = got[0:LEV, c * COLS : (c + 1) * COLS]


def spread_kernel(fields, owners, sw, s, w, o, parts, tables, aux, out, column, held):
    refs = (sw, s, w, o)
    chunk = LEV * ROWS
    total = parts[0:chunk, :]
    for f in range(1, fields):
        total = total + parts[f * chunk : (f + 1) * chunk, :]
    column[...] = total
    turned = []
    for r in range(7):
        turned.append(jnp.transpose(tables[pl.ds(r, owners, stride=ROWS), :]))
    turned = jnp.concatenate(turned, axis=0)
    turned = jnp.concatenate(split(turned, 2), axis=1)
    for half in (1, 0):
        owner = owners_of(refs, half)
        pieces = []
        for n in (0, 1):
            hot = one_hot(owner[:, n * SLOTS : (n + 1) * SLOTS], owners)
            hot = jnp.concatenate([hot, hot], axis=0)
            rows = jnp.dot(turned, hot, preferred_element_type=jnp.float32)
            sums = jnp.zeros((PADLEV, SLOTS), jnp.float32)
            for m in range(LEV):
                at = (4 * half + 2 * n) * LEV + m
                value = jnp.concatenate(
                    [column[at : at + 1, :], column[at + LEV : at + LEV + 1, :]], axis=1
                )
                sums = sums + rows[m * PADLEV : (m + 1) * PADLEV] * value
            pieces.append(sums)
        weighted = jnp.concatenate(pieces, axis=1) * weights_of(refs, half)
        hot = one_hot(place_rows(refs, half), SHIFT * COLS)
        stacked = jnp.concatenate(split(weighted, 3), axis=0)
        got = lax.dot_general(
            stacked, hot, (((1,), (1,)), ((), ())), preferred_element_type=jnp.float32
        )
        got = got[0:PADLEV] + got[PADLEV : 2 * PADLEV] + got[2 * PADLEV :]
        for r in range(SHIFT):
            held[pl.ds(SHIFT * half + r, PADLEV, stride=ROWS), :] = got[:, r * COLS : (r + 1) * COLS]
    out[0:LEV] = held[0 : LEV * ROWS, :].reshape(LEV, ROWS, COLS) * aux[0][None]
    out[LEV] = aux[1]
    out[LEV + 1] = aux[2]


def image_kernel(o, e, n, ne, d, res, image, sums):
    refs = (o, e, n, ne)
    scaled = scaled_faces(frame(refs, LEV), frame(refs, LEV + 1))
    zero = jnp.zeros((ROWS, COLS), jnp.float32)
    norm, curve, cross, square = zero, zero, zero, zero
    for g in range(LEV // GROUP):
        levels = slice(g * GROUP, (g + 1) * GROUP)
        here = d[levels]
        old = res[levels]
        x = here + north_east(diffuse(frame(refs, levels), scaled))
        image[levels] = x
        norm = norm + jnp.sum(old * old, axis=0)
        curve = curve + jnp.sum(here * x, axis=0)
        cross = cross + jnp.sum(old * x, axis=0)
        square = square + jnp.sum(x * x, axis=0)
    lane = lax.broadcasted_iota(jnp.int32, (1, COLS), 1)
    line = jnp.zeros((1, COLS), jnp.float32)
    for i, value in enumerate((norm, curve, cross, square)):
        line = jnp.where(lane == i, jnp.sum(value), line)
    sums[...] = jnp.broadcast_to(line, sums.shape)


def sum_kernel(given, out):
    out[...] = jnp.broadcast_to(jnp.sum(given[...], axis=0, keepdims=True), out.shape)


def step_kernel(given, control, res, d, image, control_next, res_next, d_next):
    line = jnp.sum(given[...], axis=0, keepdims=True)
    norm, curve, cross, square = line[:, 0:1], line[:, 1:2], line[:, 2:3], line[:, 3:4]
    alpha = norm / curve
    norm_next = jnp.maximum(norm - 2.0 * alpha * cross + alpha * alpha * square, 0.0)
    beta = norm_next / norm
    alpha = jnp.broadcast_to(alpha, (ROWS, COLS))[None]
    beta = jnp.broadcast_to(beta, (ROWS, COLS))[None]
    here = d[...]
    control_next[...] = control[...] + alpha * here
    new = res[...] - alpha * image[...]
    res_next[...] = new
    d_next[...] = new + beta * here


def call(kernel, outs, scratch=(), flops=1000000):
    whole = pl.BlockSpec(memory_space=pltpu.VMEM)
    return lambda *given: pl.pallas_call(
        kernel,
        out_shape=tuple(jax.ShapeDtypeStruct(shape, jnp.float32) for shape in outs),
        in_specs=[whole] * len(given),
        out_specs=tuple([whole] * len(outs)),
        scratch_shapes=[pltpu.VMEM(shape, jnp.float32) for shape in scratch],
        compiler_params=pltpu.CompilerParams(vmem_limit_bytes=LIMIT),
        cost_estimate=pl.CostEstimate(flops=flops, bytes_accessed=1000000, transcendentals=0),
    )(*given)


def neighbours(x, sign):
    lats, lons = lax.axis_size("lat"), lax.axis_size("lon")
    along_lat = lax.ppermute(x, "lat", [(i, (i + sign) % lats) for i in range(lats)])
    along_lon = lax.ppermute(x, "lon", [(i, (i + sign) % lons) for i in range(lons)])
    both = [
        (i * lons + j, (i + sign) % lats * lons + (j + sign) % lons)
        for i in range(lats)
        for j in range(lons)
    ]
    return along_lat, along_lon, lax.ppermute(x, ("lat", "lon"), both)


def local(
    control,
    residual,
    direction,
    land_mask,
    kappa_east,
    kappa_north,
    sigma,
    obs_weight,
    obs_cell,
    obs_owner,
    error_inverse,
):
    lats, lons, fields = lax.axis_size("lat"), lax.axis_size("lon"), lax.axis_size("obs")
    owners = lats * lons
    block = (LEV, ROWS, COLS)
    d = direction.reshape(block)
    res = residual.reshape(block)
    msg, tables = call(
        pack_kernel,
        ((M_TILES, ROWS, COLS), (owners, ROWS, COLS)),
        ((PADLEV, COLS),),
    )(
        d,
        land_mask,
        kappa_east,
        kappa_north,
        sigma.reshape(ROWS, COLS),
        obs_weight.reshape(LEV, SLOTS),
        obs_cell.reshape(2, COLS),
        obs_owner.reshape(2, COLS),
        error_inverse.reshape(LEV, LEV),
    )
    tables = lax.all_to_all(tables, ("lat", "lon"), 0, 0, tiled=True)
    south, west, both = neighbours(msg, 1)
    part, aux = call(
        pick_kernel,
        ((LEV * ROWS, COLS), (3, ROWS, COLS)),
        ((PADLEV * ROWS, COLS),),
    )(both, south, west, msg)
    parts = lax.all_gather(part, "obs", tiled=True)
    (source,) = call(
        functools.partial(spread_kernel, fields, owners),
        ((LEV + 2, ROWS, COLS),),
        ((LEV * ROWS, COLS), (PADLEV * ROWS, COLS)),
    )(both, south, west, msg, parts, tables.reshape(owners * ROWS, COLS), aux)
    north, east, both = neighbours(source, -1)
    image, sums = call(image_kernel, (block, (fields * lons, COLS)))(
        source, east, north, both, d, res
    )
    sums = lax.all_to_all(sums, ("obs", "lon"), 0, 0, tiled=True)
    (sums,) = call(sum_kernel, ((lats, COLS),))(sums)
    sums = lax.all_to_all(sums, "lat", 0, 0, tiled=True)
    outs = call(step_kernel, (block, block, block))(
        sums, control.reshape(block), res, d, image
    )
    return tuple(out.reshape(direction.shape) for out in outs)


def solution(mesh):
    state = P("obs", None, "lat", "lon")
    placed = (
        state,
        state,
        state,
        P("lat", "lon"),
        P("lat", "lon"),
        P("lat", "lon"),
        P("obs", "lat", "lon"),
        P("obs", None, ("lat", "lon")),
        P(("lat", "lon")),
        P(("lat", "lon"), None),
        P(("lat", "lon"), None, None),
    )
    return jax.shard_map(
        local, mesh=mesh, in_specs=placed, out_specs=(state, state, state), check_vma=False
    )
```

```python
import functools

import jax
import jax.numpy as jnp
from jax import lax
from jax.experimental import pallas as pl
from jax.experimental.pallas import tpu as pltpu
from jax.sharding import PartitionSpec as P

LEV = 25
PADLEV = 32
ROWS = 8
COLS = 128
SLOTS = 256
SHIFT = 4
WEST = COLS - SHIFT
SWEEPS = 4
GROUP = 5
DIAGS = LEV // 2 + 1

T_FLAG, T_EAST, T_NORTH, T_SIGMA, T_FIELDS, T_OBS = 25, 26, 27, 28, 29, 7
R_CELL, R_OWNER = 2 * LEV, 2 * LEV + 2
EDGE = 8
PER_TILE = COLS // EDGE
T_OWN = T_FIELDS + T_OBS
T_EDGES = -(-T_FIELDS // PER_TILE)
T_SIDE = T_EDGES + T_OBS
T_BAND = T_OWN + 2 * T_SIDE
T_BACK = LEV + 2
T_BACKS = T_BACK + -(-T_BACK // PER_TILE)
BLOCKS = 6
CANDIDATES = BLOCKS * SLOTS
PART_ROWS = 304
LIMIT = 48 * 1024 * 1024


def shifted(x, by, axis):
    by = by % x.shape[axis]
    return pltpu.roll(x, by, axis) if by else x


def split(x, parts):
    out = []
    for _ in range(parts):
        part = x.astype(jnp.bfloat16)
        out.append(part)
        x = x - part.astype(jnp.float32)
    return out


def lanes():
    return lax.broadcasted_iota(jnp.int32, (ROWS, COLS), 1)


def pack_edges(tiles, first):
    slot = lanes() // EDGE
    packed = []
    for start in range(0, len(tiles), PER_TILE):
        out = jnp.zeros((ROWS, COLS), jnp.float32)
        for i, tile in enumerate(tiles[start : start + PER_TILE]):
            out = jnp.where(slot == i, shifted(tile, EDGE * i - first, 1), out)
        packed.append(out)
    return packed


def frame(low, low_edge, high, high_edge):
    low = jnp.concatenate([low, low_edge], axis=-1)
    high = jnp.concatenate([high, high_edge], axis=-1)
    return jnp.concatenate([low, high], axis=-2)


def scaled_faces(ke, kn):
    kw = shifted(ke, 1, 1)
    ks = shifted(kn, 1, 0)
    inverse = 1.0 / (1.0 + ke + kw + kn + ks)
    return inverse, ke * inverse, kw * inverse, kn * inverse, ks * inverse


def diffuse(source, scaled):
    inverse, ke, kw, kn, ks = [term[None] for term in scaled]
    scaled_source = source * inverse
    x = scaled_source
    for _ in range(SWEEPS - 1):
        x = (
            scaled_source
            + ke * shifted(x, -1, 2)
            + kw * shifted(x, 1, 2)
            + kn * shifted(x, -1, 1)
            + ks * shifted(x, 1, 1)
        )
    return x


def one_hot(index, length):
    rows = lax.broadcasted_iota(jnp.int32, (length, index.shape[1]), 0)
    return jnp.where(rows == index, 1.0, 0.0).astype(jnp.bfloat16)


def side_by_side(rows):
    return jnp.concatenate([rows[0:1], rows[1:2]], axis=1)


def place(cell, south, side):
    row, col = cell // COLS, cell % COLS
    if south:
        inside = row >= ROWS - SHIFT
        row = row - (ROWS - SHIFT)
    else:
        inside = row < SHIFT
    if side == 1:
        inside = inside & (col >= WEST)
        index = row * EDGE + col - WEST
    elif side == 2:
        inside = inside & (col < SHIFT)
        index = row * EDGE + col + SHIFT
    else:
        index = row * COLS + col
    return jnp.where(inside, index, -1)


def diagonals(table, wide, turned):
    wide[...] = jnp.zeros_like(wide)
    turned[...] = jnp.zeros_like(turned)
    for i in range(LEV):
        wide[i : i + 1, 0:LEV] = table[i]
    both = wide[...]
    wide[...] = both + shifted(both, LEV, 1)
    for i in range(LEV):
        turned[i : i + 1, :] = shifted(wide[i : i + 1, :], -i, 1)
    turned[...] = jnp.transpose(turned[...])
    tile = jnp.zeros((4, COLS), jnp.float32)
    for q in range(4):
        tile = tile + shifted(turned[pl.ds(q, 4, stride=4), :], PADLEV * q, 1)
    return tile


def pack_kernel(
    d, flag, east, north, sigma, weight, cell, owner, table,
    band, to_east, to_west, tables,
    whole, lines, matrix, wide, turned, sems,
):
    obs = ROWS * T_FIELDS
    tile = lambda t: band.at[pl.ds(ROWS * t, ROWS), :]
    copies = [
        pltpu.make_async_copy(d, band.at[pl.ds(0, ROWS * LEV), :], sems.at[0]),
        pltpu.make_async_copy(flag, whole.at[pl.ds(0, ROWS), :], sems.at[1]),
        pltpu.make_async_copy(east, tile(T_EAST), sems.at[2]),
        pltpu.make_async_copy(north, tile(T_NORTH), sems.at[3]),
        pltpu.make_async_copy(sigma, tile(T_SIGMA), sems.at[4]),
        pltpu.make_async_copy(weight, lines, sems.at[5]),
        pltpu.make_async_copy(cell, whole.at[pl.ds(ROWS, 2), :], sems.at[6]),
        pltpu.make_async_copy(owner, whole.at[pl.ds(2 * ROWS, 2), :], sems.at[7]),
        pltpu.make_async_copy(table, matrix, sems.at[8]),
    ]
    for copy in copies:
        copy.start()
    for copy in copies:
        copy.wait()
    for l in range(LEV):
        for p in (0, 1):
            at = obs + 2 * l + p
            band[at : at + 1, :] = lines[l, :, p * COLS : (p + 1) * COLS]
    band[ROWS * T_FLAG : ROWS * (T_FLAG + 1), :] = whole[0:ROWS, :].astype(jnp.float32)
    band[obs + R_CELL : obs + R_CELL + 2, :] = whole[ROWS : ROWS + 2, :].astype(jnp.float32)
    band[obs + R_OWNER : obs + R_OWNER + 2, :] = whole[2 * ROWS : 2 * ROWS + 2, :].astype(jnp.float32)
    band[obs + R_OWNER + 2 : ROWS * T_OWN, :] = jnp.zeros((2, COLS), jnp.float32)
    tiles = [band[ROWS * t : ROWS * (t + 1), :] for t in range(T_FIELDS)]
    for out, first in ((to_east, COLS - EDGE), (to_west, 0)):
        for i, packed in enumerate(pack_edges(tiles, first)):
            out[ROWS * i : ROWS * (i + 1), :] = packed
        out[ROWS * T_EDGES :, :] = band[obs : ROWS * T_OWN, :]
    tile = diagonals(matrix, wide, turned)
    for i in range(tables.shape[0] // 4):
        tables[4 * i : 4 * i + 4, :] = tile


def band_kernel(band, west, east, given, out, tables):
    out[0 : ROWS * T_OWN, :] = band[...]
    out[ROWS * T_OWN : ROWS * (T_OWN + T_SIDE), :] = west[...]
    out[ROWS * (T_OWN + T_SIDE) : ROWS * T_BAND, :] = east[...]
    count = given.shape[0]
    for i in range(tables.shape[0] // count):
        tables[count * i : count * (i + 1), :] = given[...]


def pick_kernel(
    lats, lons, own, south, part, aux, weights, marks, edges, held, held_edge
):

    lane = lanes()
    for b, band in enumerate((south, own)):
        for t in range(T_FIELDS):
            at = T_OWN + t // PER_TILE
            slot = EDGE * (t % PER_TILE)
            west = band[ROWS * at : ROWS * (at + 1), :]
            east = band[ROWS * (at + T_SIDE) : ROWS * (at + T_SIDE + 1), :]
            west = shifted(west, COLS - EDGE - slot, 1)
            east = shifted(east, -slot, 1)
            edge = jnp.where(lane < EDGE, east, jnp.where(lane >= COLS - EDGE, west, 0.0))
            edges[b, t] = edge

    def framed(first, count):
        rows = slice(ROWS * first, ROWS * (first + count))
        whole = (count, ROWS, COLS)
        levels = slice(first, first + count)
        return frame(
            south[rows, :].reshape(whole), edges[0, levels], own[rows, :].reshape(whole), edges[1, levels]
        )

    flag, east, north, sigma = [framed(t, 1)[0] for t in (T_FLAG, T_EAST, T_NORTH, T_SIGMA)]
    ke = east * flag * shifted(flag, -1, 1)
    kn = north * flag * shifted(flag, -1, 0)
    row = lax.broadcasted_iota(jnp.int32, kn.shape, 0)
    kn = jnp.where((row == ROWS - 1) & (lax.axis_index("lat") == 0), 0.0, kn)
    spread = sigma * flag

    def lower(x):
        axis = x.ndim - 2
        return shifted(x, -SHIFT, axis)[..., :ROWS, :]

    for i, x in enumerate((spread, ke, kn)):
        aux[i] = lower(x)
    scaled = scaled_faces(ke, kn)
    spread = aux[0]
    held[LEV * ROWS :, :] = jnp.zeros(((PADLEV - LEV) * ROWS, COLS), jnp.float32)
    held_edge[LEV * ROWS :, :] = jnp.zeros(((PADLEV - LEV) * ROWS, COLS), jnp.float32)
    for g in range(LEV // GROUP):
        x = lower(diffuse(framed(g * GROUP, GROUP), scaled)) * spread[None]
        rows = slice(g * GROUP * ROWS, (g + 1) * GROUP * ROWS)
        held[rows, :] = x[:, :, :COLS].reshape(GROUP * ROWS, COLS)
        held_edge[rows, :] = x[:, :, COLS:].reshape(GROUP * ROWS, COLS)

    weights[LEV:, :] = jnp.zeros((PADLEV - LEV, CANDIDATES), jnp.float32)
    marks[...] = jnp.zeros_like(marks)
    for b in range(BLOCKS):
        band, side = (own, south)[b // 3], b % 3
        obs = ROWS * (T_FIELDS, T_OWN + T_EDGES, T_OWN + T_SIDE + T_EDGES)[side]
        for p in (0, 1):
            columns = slice(b * SLOTS + p * COLS, b * SLOTS + (p + 1) * COLS)
            weights[0:LEV, columns] = band[pl.ds(obs + p, LEV, stride=2), :]
        columns = slice(b * SLOTS, (b + 1) * SLOTS)
        cell = side_by_side(band[obs + R_CELL : obs + R_CELL + 2, :].astype(jnp.int32))
        marks[0:1, columns] = place(cell, b >= 3, side)
        owner = side_by_side(band[obs + R_OWNER : obs + R_OWNER + 2, :].astype(jnp.int32))
        marks[1:2, columns] = owner % lons * lats + owner // lons

    slot = lax.broadcasted_iota(jnp.int32, (PADLEV, COLS), 1) // EDGE
    for half in (0, 1):
        first = SHIFT * (1 - half)
        centre, edge = [], jnp.zeros((PADLEV, COLS), jnp.float32)
        for r in range(SHIFT):
            centre.append(held[pl.ds(first + r, PADLEV, stride=ROWS), :])
            rolled = shifted(held_edge[pl.ds(first + r, PADLEV, stride=ROWS), :], SHIFT + EDGE * r, 1)
            edge = jnp.where(slot == r, rolled, edge)
        centre = jnp.concatenate(centre, axis=1)
        base = 3 * half * SLOTS
        for state, start, width in ((centre, base, SLOTS), (edge, base + SLOTS, 2 * SLOTS)):
            hot = one_hot(marks[0:1, start : start + width], state.shape[1])
            stacked = jnp.concatenate(split(state, 3), axis=0)
            got = jnp.dot(stacked, hot, preferred_element_type=jnp.float32)
            got = got[0:PADLEV] + got[PADLEV : 2 * PADLEV] + got[2 * PADLEV :]
            got = got * weights[:, start : start + width]
            for c in range(width // COLS):
                at = (start // COLS + c) * LEV
                part[0, at : at + LEV, :] = got[0:LEV, c * COLS : (c + 1) * COLS]
    filled = 2 * BLOCKS * LEV
    part[0, filled:, :] = jnp.zeros((PART_ROWS - filled, COLS), jnp.float32)
    for f in range(1, part.shape[0]):
        part[f] = part[0]


def spread_kernel(
    fields, owners, parts, tables, weights, marks, aux, out, column, double, circled, held, held_edge
):
    total = parts[0]
    for f in range(1, fields):
        total = total + parts[f]
    column[...] = total
    rows = [jnp.transpose(tables[pl.ds(r, owners, stride=4), :]) for r in range(4)]
    rows = jnp.concatenate(rows, axis=0)
    turned = [rows[PADLEV * e : PADLEV * (e + 1)] for e in range(DIAGS)]
    double[...] = jnp.zeros_like(double)
    for e in range(DIAGS, LEV):
        other = turned[LEV - e]
        double[0:LEV, :] = other[0:LEV]
        double[LEV : 2 * LEV, :] = other[0:LEV]
        turned.append(double[e : e + PADLEV, :])
    turned = jnp.concatenate(turned, axis=0)
    turned = jnp.concatenate(split(turned, 2), axis=1)
    circled[...] = jnp.zeros_like(circled)
    weighted = []
    for b in range(BLOCKS):
        columns = slice(b * SLOTS, (b + 1) * SLOTS)
        hot = one_hot(marks[1:2, columns], owners)
        hot = jnp.concatenate([hot, hot], axis=0)
        rows = jnp.dot(turned, hot, preferred_element_type=jnp.float32)
        for p in (0, 1):
            at = (2 * b + p) * LEV
            here = column[at : at + LEV, :]
            circled[0:LEV, p * COLS : (p + 1) * COLS] = here
            circled[LEV : 2 * LEV, p * COLS : (p + 1) * COLS] = here
        sums = rows[0:PADLEV] * circled[0:PADLEV, :]
        for e in range(1, LEV):
            sums = sums + rows[PADLEV * e : PADLEV * (e + 1)] * circled[e : e + PADLEV, :]
        weighted.append(sums * weights[:, columns])
    slot = lax.broadcasted_iota(jnp.int32, (PADLEV, COLS), 1)
    inner = (slot < SHIFT) | (slot >= WEST)
    for half in (0, 1):
        first = SHIFT * (1 - half)
        centre = weighted[3 * half]
        edge = jnp.concatenate(weighted[3 * half + 1 : 3 * half + 3], axis=1)
        base = 3 * half * SLOTS
        found = []
        for value, start, length in ((centre, base, SHIFT * COLS), (edge, base + SLOTS, COLS)):
            hot = one_hot(marks[0:1, start : start + value.shape[1]], length)
            stacked = jnp.concatenate(split(value, 3), axis=0)
            got = lax.dot_general(
                stacked, hot, (((1,), (1,)), ((), ())), preferred_element_type=jnp.float32
            )
            found.append(got[0:PADLEV] + got[PADLEV : 2 * PADLEV] + got[2 * PADLEV :])
        for r in range(SHIFT):
            at = pl.ds(first + r, PADLEV, stride=ROWS)
            held[at, :] = found[0][:, r * COLS : (r + 1) * COLS]
            held_edge[at, :] = jnp.where(inner, shifted(found[1], -SHIFT - EDGE * r, 1), 0.0)
    spread = aux[0]
    tiles = []
    for t in range(LEV):
        rows = slice(ROWS * t, ROWS * (t + 1))
        out[t] = held[rows, :] * spread[:, :COLS]
        tiles.append(held_edge[rows, :] * spread[:, COLS:])
    for i in (1, 2):
        out[LEV + i - 1] = aux[i, :, :COLS]
        tiles.append(aux[i, :, COLS:])
    for i, packed in enumerate(pack_edges(tiles, WEST)):
        out[T_BACK + i] = packed


def image_kernel(own, north, d, res, image, sums, edges):
    lane = lanes()
    inner = (lane < SHIFT) | (lane >= WEST)
    for b, block in enumerate((own, north)):
        for t in range(T_BACK):
            packed = block[T_BACK + t // PER_TILE]
            edge = shifted(packed, -SHIFT - EDGE * (t % PER_TILE), 1)
            edges[b, t] = jnp.where(inner, edge, 0.0)

    def framed(levels):
        return frame(own[levels], edges[0, levels], north[levels], edges[1, levels])

    scaled = scaled_faces(framed(LEV), framed(LEV + 1))
    zero = jnp.zeros((ROWS, COLS), jnp.float32)
    norm, curve, cross, square = zero, zero, zero, zero
    for g in range(LEV // GROUP):
        levels = slice(g * GROUP, (g + 1) * GROUP)
        here = d[levels]
        old = res[levels]
        x = diffuse(framed(levels), scaled)
        x = here + shifted(x[:, :, :COLS], -SHIFT, 1)[:, :ROWS]
        image[levels] = x
        norm = norm + jnp.sum(old * old, axis=0)
        curve = curve + jnp.sum(here * x, axis=0)
        cross = cross + jnp.sum(old * x, axis=0)
        square = square + jnp.sum(x * x, axis=0)
    lane = lax.broadcasted_iota(jnp.int32, (1, COLS), 1)
    line = jnp.zeros((1, COLS), jnp.float32)
    for i, value in enumerate((norm, curve, cross, square)):
        line = jnp.where(lane == i, jnp.sum(value), line)
    sums[...] = jnp.broadcast_to(line, sums.shape)


def sum_kernel(given, out):
    out[...] = jnp.broadcast_to(jnp.sum(given[...], axis=0, keepdims=True), out.shape)


def step_kernel(given, control, res, d, image, control_next, res_next, d_next):
    line = jnp.sum(given[...], axis=0, keepdims=True)
    norm, curve, cross, square = line[:, 0:1], line[:, 1:2], line[:, 2:3], line[:, 3:4]
    alpha = norm / curve
    norm_next = jnp.maximum(norm - 2.0 * alpha * cross + alpha * alpha * square, 0.0)
    beta = norm_next / norm
    alpha = jnp.broadcast_to(alpha, (ROWS, COLS))[None]
    beta = jnp.broadcast_to(beta, (ROWS, COLS))[None]
    here = d[...]
    control_next[...] = control[...] + alpha * here
    new = res[...] - alpha * image[...]
    res_next[...] = new
    d_next[...] = new + beta * here


VMEM = pl.BlockSpec(memory_space=pltpu.VMEM)
ANY = pl.BlockSpec(memory_space=pl.ANY)


def call(kernel, outs, scratch=(), given=VMEM, limit=LIMIT, flops=1000000):
    def shape_of(out):
        shape, dtype = out if isinstance(out[1], type) else (out, jnp.float32)
        return jax.ShapeDtypeStruct(shape, dtype)

    return lambda *arrays: pl.pallas_call(
        kernel,
        out_shape=tuple(shape_of(out) for out in outs),
        in_specs=[given] * len(arrays),
        out_specs=tuple([VMEM] * len(outs)),
        scratch_shapes=[pltpu.VMEM(s, jnp.float32) if isinstance(s, tuple) else s for s in scratch],
        compiler_params=pltpu.CompilerParams(vmem_limit_bytes=limit),
        cost_estimate=pl.CostEstimate(flops=flops, bytes_accessed=1000000, transcendentals=0),
    )(*arrays)


def step(x, axis, by):
    size = lax.axis_size(axis)
    return lax.ppermute(x, axis, [(i, (i + by) % size) for i in range(size)])


def exchange(x, axis):
    size = lax.axis_size(axis)
    blocks = x.reshape(size, x.shape[0] // size, COLS)
    return lax.all_to_all(blocks, axis, 0, 0, tiled=True).reshape(x.shape)


def local(
    control,
    residual,
    direction,
    land_mask,
    kappa_east,
    kappa_north,
    sigma,
    obs_weight,
    obs_cell,
    obs_owner,
    error_inverse,
):
    lats, lons, fields = lax.axis_size("lat"), lax.axis_size("lon"), lax.axis_size("obs")
    owners = lats * lons
    block = (LEV, ROWS, COLS)
    d = direction.reshape(block)
    res = residual.reshape(block)
    band, to_east, to_west, tables = call(
        pack_kernel,
        (
            (ROWS * T_OWN, COLS),
            (ROWS * T_SIDE, COLS),
            (ROWS * T_SIDE, COLS),
            (4 * lats, COLS),
        ),
        (
            pltpu.VMEM((3 * ROWS, COLS), jnp.int32),
            (LEV, 1, SLOTS),
            (LEV, 1, LEV),
            (PADLEV, COLS),
            (COLS, COLS),
            pltpu.SemaphoreType.DMA((9,)),
        ),
        given=ANY,
        limit=56 * 1024 * 1024,
    )(
        direction.reshape(LEV * ROWS, COLS),
        land_mask,
        kappa_east,
        kappa_north,
        sigma.reshape(ROWS, COLS),
        jnp.transpose(obs_weight, (1, 0, 2)),
        obs_cell.reshape(2, COLS),
        obs_owner.reshape(2, COLS),
        jnp.transpose(error_inverse, (1, 0, 2)),
    )
    tables = exchange(tables, "lat")
    west = step(to_east, "lon", 1)
    east = step(to_west, "lon", -1)
    band, tables = call(band_kernel, ((ROWS * T_BAND, COLS), (4 * owners, COLS)))(
        band, west, east, tables
    )
    south = step(band, "lat", 1)
    tables = exchange(tables, "lon")
    part, aux, weights, marks = call(
        functools.partial(pick_kernel, lats, lons),
        (
            (fields, PART_ROWS, COLS),
            (3, ROWS, 2 * COLS),
            (PADLEV, CANDIDATES),
            ((8, CANDIDATES), jnp.int32),
        ),
        (
            (2, T_FIELDS, ROWS, COLS),
            (PADLEV * ROWS, COLS),
            (PADLEV * ROWS, COLS),
        ),
    )(band, south)
    parts = lax.all_to_all(part, "obs", 0, 0, tiled=True)
    (source,) = call(
        functools.partial(spread_kernel, fields, owners),
        ((T_BACKS, ROWS, COLS),),
        (
            (PART_ROWS, COLS),
            (2 * PADLEV, owners),
            (2 * PADLEV, SLOTS),
            (PADLEV * ROWS, COLS),
            (PADLEV * ROWS, COLS),
        ),
    )(parts, tables, weights, marks, aux)
    north = step(source, "lat", -1)
    image, sums = call(
        image_kernel, (block, (fields * lons, COLS)), ((2, T_BACK, ROWS, COLS),)
    )(source, north, d, res)
    sums = lax.all_to_all(sums, ("obs", "lon"), 0, 0, tiled=True)
    (sums,) = call(sum_kernel, ((lats, COLS),))(sums)
    sums = lax.all_to_all(sums, "lat", 0, 0, tiled=True)
    outs = call(step_kernel, (block, block, block))(sums, control.reshape(block), res, d, image)
    return tuple(out.reshape(direction.shape) for out in outs)


def solution(mesh):
    state = P("obs", None, "lat", "lon")
    placed = (
        state,
        state,
        state,
        P("lat", "lon"),
        P("lat", "lon"),
        P("lat", "lon"),
        P("obs", "lat", "lon"),
        P("obs", None, ("lat", "lon")),
        P(("lat", "lon")),
        P(("lat", "lon"), None),
        P(("lat", "lon"), None, None),
    )
    return jax.shard_map(
        local, mesh=mesh, in_specs=placed, out_specs=(state, state, state), check_vma=False
    )
```

```python
import functools

import jax
import jax.numpy as jnp
from jax import lax
from jax.experimental import pallas as pl
from jax.experimental.pallas import tpu as pltpu
from jax.sharding import PartitionSpec as P

LEV = 25
PADLEV = 32
ROWS = 8
COLS = 128
SLOTS = 256
SHIFT = 4
SWEEPS = 4
GROUP = 5
DIAGS = LEV // 2 + 1

T_FLAG, T_EAST, T_NORTH, T_SIGMA, T_FIELDS, T_OBS = 25, 26, 27, 28, 29, 7
R_CELL, R_OWNER = 2 * LEV, 2 * LEV + 2
EDGE = 8
PER_TILE = COLS // EDGE
T_OWN = T_FIELDS + T_OBS
T_EDGES = -(-T_FIELDS // PER_TILE)
T_SIDE = T_EDGES + T_OBS
T_BACK = LEV + 2
T_BACK_SIDE = -(-T_BACK // PER_TILE)
BLOCKS = 4
CANDIDATES = BLOCKS * SLOTS
PART_ROWS = 2 * BLOCKS * LEV
LIMIT = 48 * 1024 * 1024


def shifted(x, by, axis):
    by = by % x.shape[axis]
    return pltpu.roll(x, by, axis) if by else x


def split(x, parts):
    out = []
    for _ in range(parts):
        part = x.astype(jnp.bfloat16)
        out.append(part)
        x = x - part.astype(jnp.float32)
    return out


def lanes():
    return lax.broadcasted_iota(jnp.int32, (ROWS, COLS), 1)


def pack_edges(tiles, first):
    slot = lanes() // EDGE
    packed = []
    for start in range(0, len(tiles), PER_TILE):
        out = jnp.zeros((ROWS, COLS), jnp.float32)
        for i, tile in enumerate(tiles[start : start + PER_TILE]):
            out = jnp.where(slot == i, shifted(tile, EDGE * i - first, 1), out)
        packed.append(out)
    return packed


def frame(low, low_edge, high, high_edge):
    low = jnp.concatenate([low, low_edge], axis=-1)
    high = jnp.concatenate([high, high_edge], axis=-1)
    return jnp.concatenate([low, high], axis=-2)


def scaled_faces(ke, kn):
    kw = shifted(ke, 1, 1)
    ks = shifted(kn, 1, 0)
    inverse = 1.0 / (1.0 + ke + kw + kn + ks)
    return inverse, ke * inverse, kw * inverse, kn * inverse, ks * inverse


def diffuse(source, scaled):
    inverse, ke, kw, kn, ks = [term[None] for term in scaled]
    scaled_source = source * inverse
    x = scaled_source
    for _ in range(SWEEPS - 1):
        x = (
            scaled_source
            + ke * shifted(x, -1, 2)
            + kw * shifted(x, 1, 2)
            + kn * shifted(x, -1, 1)
            + ks * shifted(x, 1, 1)
        )
    return x


def one_hot(index, length):
    rows = lax.broadcasted_iota(jnp.int32, (length, index.shape[1]), 0)
    return jnp.where(rows == index, 1.0, 0.0).astype(jnp.bfloat16)


def side_by_side(rows):
    return jnp.concatenate([rows[0:1], rows[1:2]], axis=1)


def place(cell, south, west):
    row, col = cell // COLS, cell % COLS
    if south:
        inside = row >= ROWS - SHIFT
        row = row - (ROWS - SHIFT)
    else:
        inside = row < SHIFT
    if west:
        inside = inside & (col >= COLS - SHIFT)
        col = col - (COLS - SHIFT)
    else:
        inside = inside & (col < COLS - SHIFT)
        col = col + SHIFT
    return jnp.where(inside, row * COLS + col, -1)


def diagonals(table, wide, turned):
    wide[...] = jnp.zeros_like(wide)
    turned[...] = jnp.zeros_like(turned)
    for i in range(LEV):
        wide[i : i + 1, 0:LEV] = table[i]
    both = wide[...]
    wide[...] = both + shifted(both, LEV, 1)
    for i in range(LEV):
        turned[i : i + 1, :] = shifted(wide[i : i + 1, :], -i, 1)
    turned[...] = jnp.transpose(turned[...])
    tile = jnp.zeros((4, COLS), jnp.float32)
    for q in range(4):
        tile = tile + shifted(turned[pl.ds(q, 4, stride=4), :], PADLEV * q, 1)
    return tile


def pack_kernel(
    d, flag, east, north, sigma, weight, cell, owner, table,
    band, side, tile,
    whole, lines, matrix, wide, turned, sems,
):
    obs = ROWS * T_FIELDS
    place_of = lambda t: band.at[pl.ds(ROWS * t, ROWS), :]
    copies = [
        pltpu.make_async_copy(d, band.at[pl.ds(0, ROWS * LEV), :], sems.at[0]),
        pltpu.make_async_copy(flag, whole.at[pl.ds(0, ROWS), :], sems.at[1]),
        pltpu.make_async_copy(east, place_of(T_EAST), sems.at[2]),
        pltpu.make_async_copy(north, place_of(T_NORTH), sems.at[3]),
        pltpu.make_async_copy(sigma, place_of(T_SIGMA), sems.at[4]),
        pltpu.make_async_copy(weight, lines, sems.at[5]),
        pltpu.make_async_copy(cell, whole.at[pl.ds(ROWS, 2), :], sems.at[6]),
        pltpu.make_async_copy(owner, whole.at[pl.ds(2 * ROWS, 2), :], sems.at[7]),
        pltpu.make_async_copy(table, matrix, sems.at[8]),
    ]
    for copy in copies:
        copy.start()
    for copy in copies:
        copy.wait()
    for l in range(LEV):
        for p in (0, 1):
            at = obs + 2 * l + p
            band[at : at + 1, :] = lines[l, :, p * COLS : (p + 1) * COLS]
    band[ROWS * T_FLAG : ROWS * (T_FLAG + 1), :] = whole[0:ROWS, :].astype(jnp.float32)
    band[obs + R_CELL : obs + R_CELL + 2, :] = whole[ROWS : ROWS + 2, :].astype(jnp.float32)
    band[obs + R_OWNER : obs + R_OWNER + 2, :] = whole[2 * ROWS : 2 * ROWS + 2, :].astype(jnp.float32)
    band[obs + R_OWNER + 2 : ROWS * T_OWN, :] = jnp.zeros((2, COLS), jnp.float32)
    tiles = [band[ROWS * t : ROWS * (t + 1), :] for t in range(T_FIELDS)]
    for i, packed in enumerate(pack_edges(tiles, COLS - EDGE)):
        side[ROWS * i : ROWS * (i + 1), :] = packed
    side[ROWS * T_EDGES :, :] = band[obs : ROWS * T_OWN, :]
    tile[...] = diagonals(matrix, wide, turned)


def repeat_kernel(tile, tables):
    pair = jnp.concatenate([tile[...], tile[...]], axis=0)
    for i in range(tables.shape[0] // ROWS):
        tables[ROWS * i : ROWS * (i + 1), :] = pair


def pick_kernel(
    own, west, south, both, part, aux, weights, marks, edges, held
):
    lane = lanes()
    for b, side in enumerate((both, west)):
        for t in range(T_FIELDS):
            at = ROWS * (t // PER_TILE)
            packed = side[at : at + ROWS, :]
            edge = shifted(packed, COLS - EDGE - EDGE * (t % PER_TILE), 1)
            edges[b, t] = jnp.where(lane >= COLS - EDGE, edge, 0.0)

    def framed(first, count):
        rows = slice(ROWS * first, ROWS * (first + count))
        whole = (count, ROWS, COLS)
        levels = slice(first, first + count)
        return frame(
            south[rows, :].reshape(whole), edges[0, levels], own[rows, :].reshape(whole), edges[1, levels]
        )

    flag, east, north, sigma = [framed(t, 1)[0] for t in (T_FLAG, T_EAST, T_NORTH, T_SIGMA)]
    ke = east * flag * shifted(flag, -1, 1)
    kn = north * flag * shifted(flag, -1, 0)
    row = lax.broadcasted_iota(jnp.int32, kn.shape, 0)
    kn = jnp.where((row == ROWS - 1) & (lax.axis_index("lat") == 0), 0.0, kn)
    spread = sigma * flag

    def lower(x):
        axis = x.ndim - 2
        x = shifted(x, SHIFT, axis + 1)[..., :COLS]
        return shifted(x, -SHIFT, axis)[..., :ROWS, :]

    for i, x in enumerate((spread, ke, kn)):
        aux[i] = lower(x)
    scaled = scaled_faces(ke, kn)
    spread = aux[0]
    held[LEV * ROWS :, :] = jnp.zeros(((PADLEV - LEV) * ROWS, COLS), jnp.float32)
    for g in range(LEV // GROUP):
        x = lower(diffuse(framed(g * GROUP, GROUP), scaled)) * spread[None]
        rows = slice(g * GROUP * ROWS, (g + 1) * GROUP * ROWS)
        held[rows, :] = x.reshape(GROUP * ROWS, COLS)

    weights[LEV:, :] = jnp.zeros((PADLEV - LEV, CANDIDATES), jnp.float32)
    marks[...] = jnp.zeros_like(marks)
    for b in range(BLOCKS):
        band = (own, west, south, both)[b]
        obs = ROWS * (T_EDGES if b % 2 else T_FIELDS)
        for p in (0, 1):
            columns = slice(b * SLOTS + p * COLS, b * SLOTS + (p + 1) * COLS)
            weights[0:LEV, columns] = band[pl.ds(obs + p, LEV, stride=2), :]
        columns = slice(b * SLOTS, (b + 1) * SLOTS)
        cell = side_by_side(band[obs + R_CELL : obs + R_CELL + 2, :].astype(jnp.int32))
        marks[0:1, columns] = place(cell, b >= 2, b % 2)
        owner = side_by_side(band[obs + R_OWNER : obs + R_OWNER + 2, :].astype(jnp.int32))
        marks[1:2, columns] = owner

    for half in (0, 1):
        first = SHIFT * (1 - half)
        state = jnp.concatenate(
            [held[pl.ds(first + r, PADLEV, stride=ROWS), :] for r in range(SHIFT)], axis=1
        )
        columns = slice(2 * half * SLOTS, 2 * (half + 1) * SLOTS)
        hot = one_hot(marks[0:1, columns], SHIFT * COLS)
        stacked = jnp.concatenate(split(state, 3), axis=0)
        got = jnp.dot(stacked, hot, preferred_element_type=jnp.float32)
        got = got[0:PADLEV] + got[PADLEV : 2 * PADLEV] + got[2 * PADLEV :]
        got = got * weights[:, columns]
        for c in range(4):
            at = (4 * half + c) * LEV
            part[at : at + LEV, :] = got[0:LEV, c * COLS : (c + 1) * COLS]


def spread_kernel(
    fields, owners, parts, tables, weights, marks, aux, out, side, column, double, circled, held
):
    total = parts[0:PART_ROWS, :]
    for f in range(1, fields):
        total = total + parts[f * PART_ROWS : (f + 1) * PART_ROWS, :]
    column[...] = total
    rows = [jnp.transpose(tables[pl.ds(r, owners, stride=4), :]) for r in range(4)]
    rows = jnp.concatenate(rows, axis=0)
    turned = [rows[PADLEV * e : PADLEV * (e + 1)] for e in range(DIAGS)]
    double[...] = jnp.zeros_like(double)
    for e in range(DIAGS, LEV):
        other = turned[LEV - e]
        double[0:LEV, :] = other[0:LEV]
        double[LEV : 2 * LEV, :] = other[0:LEV]
        turned.append(double[e : e + PADLEV, :])
    turned = jnp.concatenate(turned, axis=0)
    turned = jnp.concatenate(split(turned, 2), axis=1)
    circled[...] = jnp.zeros_like(circled)
    weighted = []
    for b in range(BLOCKS):
        columns = slice(b * SLOTS, (b + 1) * SLOTS)
        hot = one_hot(marks[1:2, columns], owners)
        hot = jnp.concatenate([hot, hot], axis=0)
        rows = jnp.dot(turned, hot, preferred_element_type=jnp.float32)
        for p in (0, 1):
            at = (2 * b + p) * LEV
            here = column[at : at + LEV, :]
            circled[0:LEV, p * COLS : (p + 1) * COLS] = here
            circled[LEV : 2 * LEV, p * COLS : (p + 1) * COLS] = here
        sums = rows[0:PADLEV] * circled[0:PADLEV, :]
        for e in range(1, LEV):
            sums = sums + rows[PADLEV * e : PADLEV * (e + 1)] * circled[e : e + PADLEV, :]
        weighted.append(sums * weights[:, columns])
    for half in (0, 1):
        first = SHIFT * (1 - half)
        value = jnp.concatenate(weighted[2 * half : 2 * half + 2], axis=1)
        columns = slice(2 * half * SLOTS, 2 * (half + 1) * SLOTS)
        hot = one_hot(marks[0:1, columns], SHIFT * COLS)
        stacked = jnp.concatenate(split(value, 3), axis=0)
        got = lax.dot_general(
            stacked, hot, (((1,), (1,)), ((), ())), preferred_element_type=jnp.float32
        )
        got = got[0:PADLEV] + got[PADLEV : 2 * PADLEV] + got[2 * PADLEV :]
        for r in range(SHIFT):
            held[pl.ds(first + r, PADLEV, stride=ROWS), :] = got[:, r * COLS : (r + 1) * COLS]
    tiles = [held[ROWS * t : ROWS * (t + 1), :] * aux[0] for t in range(LEV)] + [aux[1], aux[2]]
    for t, tile in enumerate(tiles):
        out[t] = tile
    for i, packed in enumerate(pack_edges(tiles, 0)):
        side[i] = packed


def image_kernel(own, east, north, both, d, res, image, sums, edges):
    lane = lanes()
    for b, side in enumerate((east, both)):
        for t in range(T_BACK):
            edge = shifted(side[t // PER_TILE], -EDGE * (t % PER_TILE), 1)
            edges[b, t] = jnp.where(lane < EDGE, edge, 0.0)

    def framed(levels):
        return frame(own[levels], edges[0, levels], north[levels], edges[1, levels])

    scaled = scaled_faces(framed(LEV), framed(LEV + 1))
    zero = jnp.zeros((ROWS, COLS), jnp.float32)
    norm, curve, cross, square = zero, zero, zero, zero
    for g in range(LEV // GROUP):
        levels = slice(g * GROUP, (g + 1) * GROUP)
        here = d[levels]
        old = res[levels]
        x = diffuse(framed(levels), scaled)
        x = shifted(x, -SHIFT, 2)[:, :, :COLS]
        x = here + shifted(x, -SHIFT, 1)[:, :ROWS]
        image[levels] = x
        norm = norm + jnp.sum(old * old, axis=0)
        curve = curve + jnp.sum(here * x, axis=0)
        cross = cross + jnp.sum(old * x, axis=0)
        square = square + jnp.sum(x * x, axis=0)
    lane = lax.broadcasted_iota(jnp.int32, (1, COLS), 1)
    line = jnp.zeros((1, COLS), jnp.float32)
    for i, value in enumerate((norm, curve, cross, square)):
        line = jnp.where(lane == i, jnp.sum(value), line)
    sums[...] = jnp.broadcast_to(line, sums.shape)


def sum_kernel(given, out):
    out[...] = jnp.broadcast_to(jnp.sum(given[...], axis=0, keepdims=True), out.shape)


def step_kernel(given, control, res, d, image, control_next, res_next, d_next):
    line = jnp.sum(given[...], axis=0, keepdims=True)
    norm, curve, cross, square = line[:, 0:1], line[:, 1:2], line[:, 2:3], line[:, 3:4]
    alpha = norm / curve
    norm_next = jnp.maximum(norm - 2.0 * alpha * cross + alpha * alpha * square, 0.0)
    beta = norm_next / norm
    alpha = jnp.broadcast_to(alpha, (ROWS, COLS))[None]
    beta = jnp.broadcast_to(beta, (ROWS, COLS))[None]
    here = d[...]
    control_next[...] = control[...] + alpha * here
    new = res[...] - alpha * image[...]
    res_next[...] = new
    d_next[...] = new + beta * here


VMEM = pl.BlockSpec(memory_space=pltpu.VMEM)
ANY = pl.BlockSpec(memory_space=pl.ANY)


def call(kernel, outs, scratch=(), given=VMEM, limit=LIMIT, flops=1000000):
    def shape_of(out):
        shape, dtype = out if isinstance(out[1], type) else (out, jnp.float32)
        return jax.ShapeDtypeStruct(shape, dtype)

    return lambda *arrays: pl.pallas_call(
        kernel,
        out_shape=tuple(shape_of(out) for out in outs),
        in_specs=[given] * len(arrays),
        out_specs=tuple([VMEM] * len(outs)),
        scratch_shapes=[pltpu.VMEM(s, jnp.float32) if isinstance(s, tuple) else s for s in scratch],
        compiler_params=pltpu.CompilerParams(vmem_limit_bytes=limit),
        cost_estimate=pl.CostEstimate(flops=flops, bytes_accessed=1000000, transcendentals=0),
    )(*arrays)


def step(x, axis, by):
    size = lax.axis_size(axis)
    return lax.ppermute(x, axis, [(i, (i + by) % size) for i in range(size)])


def step_both(x, by):
    lats, lons = lax.axis_size("lat"), lax.axis_size("lon")
    pairs = [
        (i * lons + j, (i + by) % lats * lons + (j + by) % lons)
        for i in range(lats)
        for j in range(lons)
    ]
    return lax.ppermute(x, ("lat", "lon"), pairs)


def local(
    control,
    residual,
    direction,
    land_mask,
    kappa_east,
    kappa_north,
    sigma,
    obs_weight,
    obs_cell,
    obs_owner,
    error_inverse,
):
    lats, lons, fields = lax.axis_size("lat"), lax.axis_size("lon"), lax.axis_size("obs")
    owners = lats * lons
    block = (LEV, ROWS, COLS)
    d = direction.reshape(block)
    res = residual.reshape(block)
    own, side, tile = call(
        pack_kernel,
        (
            (ROWS * T_OWN, COLS),
            (ROWS * T_SIDE, COLS),
            (4, COLS),
        ),
        (
            pltpu.VMEM((3 * ROWS, COLS), jnp.int32),
            (LEV, 1, SLOTS),
            (LEV, 1, LEV),
            (PADLEV, COLS),
            (COLS, COLS),
            pltpu.SemaphoreType.DMA((9,)),
        ),
        given=ANY,
        limit=56 * 1024 * 1024,
    )(
        direction.reshape(LEV * ROWS, COLS),
        land_mask,
        kappa_east,
        kappa_north,
        sigma.reshape(ROWS, COLS),
        jnp.transpose(obs_weight, (1, 0, 2)),
        obs_cell.reshape(2, COLS),
        obs_owner.reshape(2, COLS),
        jnp.transpose(error_inverse, (1, 0, 2)),
    )
    south = step(own, "lat", 1)
    west = step(side, "lon", 1)
    both = step_both(side, 1)
    (tables,) = call(repeat_kernel, ((4 * owners, COLS),))(tile)
    tables = lax.all_to_all(
        tables.reshape(owners, 4, COLS), ("lat", "lon"), 0, 0, tiled=True
    ).reshape(4 * owners, COLS)
    part, aux, weights, marks = call(
        pick_kernel,
        (
            (PART_ROWS, COLS),
            (3, ROWS, COLS),
            (PADLEV, CANDIDATES),
            ((8, CANDIDATES), jnp.int32),
        ),
        ((2, T_FIELDS, ROWS, COLS), (PADLEV * ROWS, COLS)),
        flops=20000000000,
    )(own, west, south, both)
    parts = lax.all_gather(part, "obs", tiled=True)
    source, side = call(
        functools.partial(spread_kernel, fields, owners),
        ((T_BACK, ROWS, COLS), (T_BACK_SIDE, ROWS, COLS)),
        (
            (PART_ROWS, COLS),
            (2 * PADLEV, owners),
            (2 * PADLEV, SLOTS),
            (PADLEV * ROWS, COLS),
        ),
    )(parts, tables, weights, marks, aux)
    north = step(source, "lat", -1)
    east = step(side, "lon", -1)
    both = step_both(side, -1)
    image, sums = call(
        image_kernel, (block, (fields * lons, COLS)), ((2, T_BACK, ROWS, COLS),)
    )(source, east, north, both, d, res)
    sums = lax.all_to_all(sums, ("obs", "lon"), 0, 0, tiled=True)
    (sums,) = call(sum_kernel, ((lats, COLS),))(sums)
    sums = lax.all_to_all(sums, "lat", 0, 0, tiled=True)
    outs = call(step_kernel, (block, block, block))(sums, control.reshape(block), res, d, image)
    return tuple(out.reshape(direction.shape) for out in outs)


def solution(mesh):
    state = P("obs", None, "lat", "lon")
    placed = (
        state,
        state,
        state,
        P("lat", "lon"),
        P("lat", "lon"),
        P("lat", "lon"),
        P("obs", "lat", "lon"),
        P("obs", None, ("lat", "lon")),
        P(("lat", "lon")),
        P(("lat", "lon"), None),
        P(("lat", "lon"), None, None),
    )
    return jax.shard_map(
        local, mesh=mesh, in_specs=placed, out_specs=(state, state, state), check_vma=False
    )
```

```python
import functools

import jax
import jax.numpy as jnp
from jax import lax
from jax.experimental import pallas as pl
from jax.experimental.pallas import tpu as pltpu
from jax.sharding import PartitionSpec as P

LEV = 25
PADLEV = 32
ROWS = 8
COLS = 128
SLOTS = 256
SHIFT = 4
SWEEPS = 4
GROUP = 5
DIAGS = LEV // 2 + 1

T_FLAG, T_EAST, T_NORTH, T_SIGMA, T_FIELDS, T_OBS = 25, 26, 27, 28, 29, 7
R_CELL, R_OWNER = 2 * LEV, 2 * LEV + 2
EDGE = 8
PER_TILE = COLS // EDGE
T_OWN = T_FIELDS + T_OBS
T_EDGES = -(-T_FIELDS // PER_TILE)
T_SIDE = T_EDGES + T_OBS
T_BACK = LEV + 2
T_BACK_SIDE = -(-T_BACK // PER_TILE)
BLOCKS = 4
CANDIDATES = BLOCKS * SLOTS
PART_ROWS = 2 * BLOCKS * LEV
LIMIT = 48 * 1024 * 1024


def shifted(x, by, axis):
    by = by % x.shape[axis]
    return pltpu.roll(x, by, axis) if by else x


def split(x, parts):
    out = []
    for _ in range(parts):
        part = x.astype(jnp.bfloat16)
        out.append(part)
        x = x - part.astype(jnp.float32)
    return out


def lanes():
    return lax.broadcasted_iota(jnp.int32, (ROWS, COLS), 1)


def pack_edges(tiles, first):
    slot = lanes() // EDGE
    packed = []
    for start in range(0, len(tiles), PER_TILE):
        out = jnp.zeros((ROWS, COLS), jnp.float32)
        for i, tile in enumerate(tiles[start : start + PER_TILE]):
            out = jnp.where(slot == i, shifted(tile, EDGE * i - first, 1), out)
        packed.append(out)
    return packed


def frame(low, low_edge, high, high_edge):
    low = jnp.concatenate([low, low_edge], axis=-1)
    high = jnp.concatenate([high, high_edge], axis=-1)
    return jnp.concatenate([low, high], axis=-2)


def scaled_faces(ke, kn):
    kw = shifted(ke, 1, 1)
    ks = shifted(kn, 1, 0)
    inverse = 1.0 / (1.0 + ke + kw + kn + ks)
    return inverse, ke * inverse, kw * inverse, kn * inverse, ks * inverse


def diffuse(source, scaled):
    inverse, ke, kw, kn, ks = [term[None] for term in scaled]
    scaled_source = source * inverse
    x = scaled_source
    for _ in range(SWEEPS - 1):
        x = (
            scaled_source
            + ke * shifted(x, -1, 2)
            + kw * shifted(x, 1, 2)
            + kn * shifted(x, -1, 1)
            + ks * shifted(x, 1, 1)
        )
    return x


def one_hot(index, length):
    rows = lax.broadcasted_iota(jnp.int32, (length, index.shape[1]), 0)
    return jnp.where(rows == index, 1.0, 0.0).astype(jnp.bfloat16)


def side_by_side(rows):
    return jnp.concatenate([rows[0:1], rows[1:2]], axis=1)


def place(cell, south, west):
    row, col = cell // COLS, cell % COLS
    if south:
        inside = row >= ROWS - SHIFT
        row = row - (ROWS - SHIFT)
    else:
        inside = row < SHIFT
    if west:
        inside = inside & (col >= COLS - SHIFT)
        col = col - (COLS - SHIFT)
    else:
        inside = inside & (col < COLS - SHIFT)
        col = col + SHIFT
    return jnp.where(inside, row * COLS + col, -1)


def diagonals(table, wide, turned):
    wide[...] = jnp.zeros_like(wide)
    turned[...] = jnp.zeros_like(turned)
    for i in range(LEV):
        wide[i : i + 1, 0:LEV] = table[i]
    both = wide[...]
    wide[...] = both + shifted(both, LEV, 1)
    for i in range(LEV):
        turned[i : i + 1, :] = shifted(wide[i : i + 1, :], -i, 1)
    turned[...] = jnp.transpose(turned[...])
    tile = jnp.zeros((4, COLS), jnp.float32)
    for q in range(4):
        tile = tile + shifted(turned[pl.ds(q, 4, stride=4), :], PADLEV * q, 1)
    return tile


def pack_kernel(
    d, flag, east, north, sigma, weight, cell, owner, table,
    band, side, tables,
    whole, lines, matrix, wide, turned, sems,
):
    obs = ROWS * T_FIELDS
    place_of = lambda t: band.at[pl.ds(ROWS * t, ROWS), :]
    copies = [
        pltpu.make_async_copy(d, band.at[pl.ds(0, ROWS * LEV), :], sems.at[0]),
        pltpu.make_async_copy(flag, whole.at[pl.ds(0, ROWS), :], sems.at[1]),
        pltpu.make_async_copy(east, place_of(T_EAST), sems.at[2]),
        pltpu.make_async_copy(north, place_of(T_NORTH), sems.at[3]),
        pltpu.make_async_copy(sigma, place_of(T_SIGMA), sems.at[4]),
        pltpu.make_async_copy(weight, lines, sems.at[5]),
        pltpu.make_async_copy(cell, whole.at[pl.ds(ROWS, 2), :], sems.at[6]),
        pltpu.make_async_copy(owner, whole.at[pl.ds(2 * ROWS, 2), :], sems.at[7]),
        pltpu.make_async_copy(table, matrix, sems.at[8]),
    ]
    for copy in copies:
        copy.start()
    for copy in copies:
        copy.wait()
    for l in range(LEV):
        for p in (0, 1):
            at = obs + 2 * l + p
            band[at : at + 1, :] = lines[l, :, p * COLS : (p + 1) * COLS]
    band[ROWS * T_FLAG : ROWS * (T_FLAG + 1), :] = whole[0:ROWS, :].astype(jnp.float32)
    band[obs + R_CELL : obs + R_CELL + 2, :] = whole[ROWS : ROWS + 2, :].astype(jnp.float32)
    band[obs + R_OWNER : obs + R_OWNER + 2, :] = whole[2 * ROWS : 2 * ROWS + 2, :].astype(jnp.float32)
    band[obs + R_OWNER + 2 : ROWS * T_OWN, :] = jnp.zeros((2, COLS), jnp.float32)
    tiles = [band[ROWS * t : ROWS * (t + 1), :] for t in range(T_FIELDS)]
    for i, packed in enumerate(pack_edges(tiles, COLS - EDGE)):
        side[ROWS * i : ROWS * (i + 1), :] = packed
    side[ROWS * T_EDGES :, :] = band[obs : ROWS * T_OWN, :]
    tile = diagonals(matrix, wide, turned)
    for i in range(tables.shape[0] // 4):
        tables[4 * i : 4 * i + 4, :] = tile


def band_kernel(given, west, out, sem):
    del given
    copy = pltpu.make_async_copy(west, out.at[pl.ds(ROWS * T_OWN, ROWS * T_SIDE), :], sem)
    copy.start()
    copy.wait()


def repeat_kernel(given, tables):
    count = given.shape[0]
    for i in range(tables.shape[0] // count):
        tables[count * i : count * (i + 1), :] = given[...]


def pick_kernel(lats, lons, own, south, part, aux, weights, marks, edges, held):
    west = own.at[pl.ds(ROWS * T_OWN, ROWS * T_SIDE), :]
    both = south.at[pl.ds(ROWS * T_OWN, ROWS * T_SIDE), :]
    lane = lanes()
    for b, side in enumerate((both, west)):
        for t in range(T_FIELDS):
            at = ROWS * (t // PER_TILE)
            packed = side[at : at + ROWS, :]
            edge = shifted(packed, COLS - EDGE - EDGE * (t % PER_TILE), 1)
            edges[b, t] = jnp.where(lane >= COLS - EDGE, edge, 0.0)

    def framed(first, count):
        rows = slice(ROWS * first, ROWS * (first + count))
        whole = (count, ROWS, COLS)
        levels = slice(first, first + count)
        return frame(
            south[rows, :].reshape(whole), edges[0, levels], own[rows, :].reshape(whole), edges[1, levels]
        )

    flag, east, north, sigma = [framed(t, 1)[0] for t in (T_FLAG, T_EAST, T_NORTH, T_SIGMA)]
    ke = east * flag * shifted(flag, -1, 1)
    kn = north * flag * shifted(flag, -1, 0)
    row = lax.broadcasted_iota(jnp.int32, kn.shape, 0)
    kn = jnp.where((row == ROWS - 1) & (lax.axis_index("lat") == 0), 0.0, kn)
    spread = sigma * flag

    def lower(x):
        axis = x.ndim - 2
        x = shifted(x, SHIFT, axis + 1)[..., :COLS]
        return shifted(x, -SHIFT, axis)[..., :ROWS, :]

    for i, x in enumerate((spread, ke, kn)):
        aux[i] = lower(x)
    scaled = scaled_faces(ke, kn)
    spread = aux[0]
    held[LEV * ROWS :, :] = jnp.zeros(((PADLEV - LEV) * ROWS, COLS), jnp.float32)
    for g in range(LEV // GROUP):
        x = lower(diffuse(framed(g * GROUP, GROUP), scaled)) * spread[None]
        rows = slice(g * GROUP * ROWS, (g + 1) * GROUP * ROWS)
        held[rows, :] = x.reshape(GROUP * ROWS, COLS)

    weights[LEV:, :] = jnp.zeros((PADLEV - LEV, CANDIDATES), jnp.float32)
    marks[...] = jnp.zeros_like(marks)
    for b in range(BLOCKS):
        band = (own, west, south, both)[b]
        obs = ROWS * (T_EDGES if b % 2 else T_FIELDS)
        for p in (0, 1):
            columns = slice(b * SLOTS + p * COLS, b * SLOTS + (p + 1) * COLS)
            weights[0:LEV, columns] = band[pl.ds(obs + p, LEV, stride=2), :]
        columns = slice(b * SLOTS, (b + 1) * SLOTS)
        cell = side_by_side(band[obs + R_CELL : obs + R_CELL + 2, :].astype(jnp.int32))
        marks[0:1, columns] = place(cell, b >= 2, b % 2)
        owner = side_by_side(band[obs + R_OWNER : obs + R_OWNER + 2, :].astype(jnp.int32))
        marks[1:2, columns] = owner % lons * lats + owner // lons

    for half in (0, 1):
        first = SHIFT * (1 - half)
        state = jnp.concatenate(
            [held[pl.ds(first + r, PADLEV, stride=ROWS), :] for r in range(SHIFT)], axis=1
        )
        columns = slice(2 * half * SLOTS, 2 * (half + 1) * SLOTS)
        hot = one_hot(marks[0:1, columns], SHIFT * COLS)
        stacked = jnp.concatenate(split(state, 3), axis=0)
        got = jnp.dot(stacked, hot, preferred_element_type=jnp.float32)
        got = got[0:PADLEV] + got[PADLEV : 2 * PADLEV] + got[2 * PADLEV :]
        got = got * weights[:, columns]
        for c in range(4):
            at = (4 * half + c) * LEV
            part[at : at + LEV, :] = got[0:LEV, c * COLS : (c + 1) * COLS]


def spread_kernel(
    fields, owners, parts, tables, weights, marks, aux, out, side, column, double, circled, held
):
    total = parts[0:PART_ROWS, :]
    for f in range(1, fields):
        total = total + parts[f * PART_ROWS : (f + 1) * PART_ROWS, :]
    column[...] = total
    rows = [jnp.transpose(tables[pl.ds(r, owners, stride=4), :]) for r in range(4)]
    rows = jnp.concatenate(rows, axis=0)
    turned = [rows[PADLEV * e : PADLEV * (e + 1)] for e in range(DIAGS)]
    double[...] = jnp.zeros_like(double)
    for e in range(DIAGS, LEV):
        other = turned[LEV - e]
        double[0:LEV, :] = other[0:LEV]
        double[LEV : 2 * LEV, :] = other[0:LEV]
        turned.append(double[e : e + PADLEV, :])
    turned = jnp.concatenate(turned, axis=0)
    turned = jnp.concatenate(split(turned, 2), axis=1)
    circled[...] = jnp.zeros_like(circled)
    weighted = []
    for b in range(BLOCKS):
        columns = slice(b * SLOTS, (b + 1) * SLOTS)
        hot = one_hot(marks[1:2, columns], owners)
        hot = jnp.concatenate([hot, hot], axis=0)
        rows = jnp.dot(turned, hot, preferred_element_type=jnp.float32)
        for p in (0, 1):
            at = (2 * b + p) * LEV
            here = column[at : at + LEV, :]
            circled[0:LEV, p * COLS : (p + 1) * COLS] = here
            circled[LEV : 2 * LEV, p * COLS : (p + 1) * COLS] = here
        sums = rows[0:PADLEV] * circled[0:PADLEV, :]
        for e in range(1, LEV):
            sums = sums + rows[PADLEV * e : PADLEV * (e + 1)] * circled[e : e + PADLEV, :]
        weighted.append(sums * weights[:, columns])
    for half in (0, 1):
        first = SHIFT * (1 - half)
        value = jnp.concatenate(weighted[2 * half : 2 * half + 2], axis=1)
        columns = slice(2 * half * SLOTS, 2 * (half + 1) * SLOTS)
        hot = one_hot(marks[0:1, columns], SHIFT * COLS)
        stacked = jnp.concatenate(split(value, 3), axis=0)
        got = lax.dot_general(
            stacked, hot, (((1,), (1,)), ((), ())), preferred_element_type=jnp.float32
        )
        got = got[0:PADLEV] + got[PADLEV : 2 * PADLEV] + got[2 * PADLEV :]
        for r in range(SHIFT):
            held[pl.ds(first + r, PADLEV, stride=ROWS), :] = got[:, r * COLS : (r + 1) * COLS]
    tiles = [held[ROWS * t : ROWS * (t + 1), :] * aux[0] for t in range(LEV)] + [aux[1], aux[2]]
    for t, tile in enumerate(tiles):
        out[t] = tile
    for i, packed in enumerate(pack_edges(tiles, 0)):
        side[i] = packed


def image_kernel(own, east, north, both, d, res, image, sums, edges):
    lane = lanes()
    for b, side in enumerate((east, both)):
        for t in range(T_BACK):
            edge = shifted(side[t // PER_TILE], -EDGE * (t % PER_TILE), 1)
            edges[b, t] = jnp.where(lane < EDGE, edge, 0.0)

    def framed(levels):
        return frame(own[levels], edges[0, levels], north[levels], edges[1, levels])

    scaled = scaled_faces(framed(LEV), framed(LEV + 1))
    zero = jnp.zeros((ROWS, COLS), jnp.float32)
    norm, curve, cross, square = zero, zero, zero, zero
    for g in range(LEV // GROUP):
        levels = slice(g * GROUP, (g + 1) * GROUP)
        here = d[levels]
        old = res[levels]
        x = diffuse(framed(levels), scaled)
        x = shifted(x, -SHIFT, 2)[:, :, :COLS]
        x = here + shifted(x, -SHIFT, 1)[:, :ROWS]
        image[levels] = x
        norm = norm + jnp.sum(old * old, axis=0)
        curve = curve + jnp.sum(here * x, axis=0)
        cross = cross + jnp.sum(old * x, axis=0)
        square = square + jnp.sum(x * x, axis=0)
    lane = lax.broadcasted_iota(jnp.int32, (1, COLS), 1)
    line = jnp.zeros((1, COLS), jnp.float32)
    for i, value in enumerate((norm, curve, cross, square)):
        line = jnp.where(lane == i, jnp.sum(value), line)
    sums[...] = jnp.broadcast_to(line, sums.shape)


def sum_kernel(given, out):
    out[...] = jnp.broadcast_to(jnp.sum(given[...], axis=0, keepdims=True), out.shape)


def step_kernel(given, control, res, d, image, control_next, res_next, d_next):
    line = jnp.sum(given[...], axis=0, keepdims=True)
    norm, curve, cross, square = line[:, 0:1], line[:, 1:2], line[:, 2:3], line[:, 3:4]
    alpha = norm / curve
    norm_next = jnp.maximum(norm - 2.0 * alpha * cross + alpha * alpha * square, 0.0)
    beta = norm_next / norm
    alpha = jnp.broadcast_to(alpha, (ROWS, COLS))[None]
    beta = jnp.broadcast_to(beta, (ROWS, COLS))[None]
    here = d[...]
    control_next[...] = control[...] + alpha * here
    new = res[...] - alpha * image[...]
    res_next[...] = new
    d_next[...] = new + beta * here


VMEM = pl.BlockSpec(memory_space=pltpu.VMEM)
ANY = pl.BlockSpec(memory_space=pl.ANY)


def call(kernel, outs, scratch=(), given=VMEM, limit=LIMIT, flops=1000000):
    def shape_of(out):
        shape, dtype = out if isinstance(out[1], type) else (out, jnp.float32)
        return jax.ShapeDtypeStruct(shape, dtype)

    return lambda *arrays: pl.pallas_call(
        kernel,
        out_shape=tuple(shape_of(out) for out in outs),
        in_specs=[given] * len(arrays),
        out_specs=tuple([VMEM] * len(outs)),
        scratch_shapes=[pltpu.VMEM(s, jnp.float32) if isinstance(s, tuple) else s for s in scratch],
        compiler_params=pltpu.CompilerParams(vmem_limit_bytes=limit),
        cost_estimate=pl.CostEstimate(flops=flops, bytes_accessed=1000000, transcendentals=0),
    )(*arrays)


def step(x, axis, by):
    size = lax.axis_size(axis)
    return lax.ppermute(x, axis, [(i, (i + by) % size) for i in range(size)])


def exchange(x, axis):
    size = lax.axis_size(axis)
    blocks = x.reshape(size, x.shape[0] // size, COLS)
    return lax.all_to_all(blocks, axis, 0, 0, tiled=True).reshape(x.shape)


def step_both(x, by):
    lats, lons = lax.axis_size("lat"), lax.axis_size("lon")
    pairs = [
        (i * lons + j, (i + by) % lats * lons + (j + by) % lons)
        for i in range(lats)
        for j in range(lons)
    ]
    return lax.ppermute(x, ("lat", "lon"), pairs)


def local(
    control,
    residual,
    direction,
    land_mask,
    kappa_east,
    kappa_north,
    sigma,
    obs_weight,
    obs_cell,
    obs_owner,
    error_inverse,
):
    lats, lons, fields = lax.axis_size("lat"), lax.axis_size("lon"), lax.axis_size("obs")
    owners = lats * lons
    block = (LEV, ROWS, COLS)
    d = direction.reshape(block)
    res = residual.reshape(block)
    own, side, tables = call(
        pack_kernel,
        (
            (ROWS * (T_OWN + T_SIDE), COLS),
            (ROWS * T_SIDE, COLS),
            (4 * lats, COLS),
        ),
        (
            pltpu.VMEM((3 * ROWS, COLS), jnp.int32),
            (LEV, 1, SLOTS),
            (LEV, 1, LEV),
            (PADLEV, COLS),
            (COLS, COLS),
            pltpu.SemaphoreType.DMA((9,)),
        ),
        given=ANY,
        limit=56 * 1024 * 1024,
    )(
        direction.reshape(LEV * ROWS, COLS),
        land_mask,
        kappa_east,
        kappa_north,
        sigma.reshape(ROWS, COLS),
        jnp.transpose(obs_weight, (1, 0, 2)),
        obs_cell.reshape(2, COLS),
        obs_owner.reshape(2, COLS),
        jnp.transpose(error_inverse, (1, 0, 2)),
    )
    west = step(side, "lon", 1)
    tables = exchange(tables, "lat")
    band = pl.pallas_call(
        band_kernel,
        out_shape=jax.ShapeDtypeStruct(own.shape, jnp.float32),
        in_specs=[ANY, ANY],
        out_specs=ANY,
        scratch_shapes=[pltpu.SemaphoreType.DMA],
        input_output_aliases={0: 0},
        compiler_params=pltpu.CompilerParams(vmem_limit_bytes=LIMIT),
    )(own, west)
    south = step(band, "lat", 1)
    (tables,) = call(repeat_kernel, ((4 * owners, COLS),), flops=20000000000)(tables)
    tables = exchange(tables, "lon")
    part, aux, weights, marks = call(
        functools.partial(pick_kernel, lats, lons),
        (
            (PART_ROWS, COLS),
            (3, ROWS, COLS),
            (PADLEV, CANDIDATES),
            ((8, CANDIDATES), jnp.int32),
        ),
        ((2, T_FIELDS, ROWS, COLS), (PADLEV * ROWS, COLS)),
        flops=20000000000,
    )(band, south)
    parts = lax.all_gather(part, "obs", tiled=True)
    source, side = call(
        functools.partial(spread_kernel, fields, owners),
        ((T_BACK, ROWS, COLS), (T_BACK_SIDE, ROWS, COLS)),
        (
            (PART_ROWS, COLS),
            (2 * PADLEV, owners),
            (2 * PADLEV, SLOTS),
            (PADLEV * ROWS, COLS),
        ),
    )(parts, tables, weights, marks, aux)
    north = step(source, "lat", -1)
    east = step(side, "lon", -1)
    both = step_both(side, -1)
    image, sums = call(
        image_kernel, (block, (fields * lons, COLS)), ((2, T_BACK, ROWS, COLS),)
    )(source, east, north, both, d, res)
    sums = lax.all_to_all(sums, ("obs", "lon"), 0, 0, tiled=True)
    (sums,) = call(sum_kernel, ((lats, COLS),))(sums)
    sums = lax.all_to_all(sums, "lat", 0, 0, tiled=True)
    outs = call(step_kernel, (block, block, block))(sums, control.reshape(block), res, d, image)
    return tuple(out.reshape(direction.shape) for out in outs)


def solution(mesh):
    state = P("obs", None, "lat", "lon")
    placed = (
        state,
        state,
        state,
        P("lat", "lon"),
        P("lat", "lon"),
        P("lat", "lon"),
        P("obs", "lat", "lon"),
        P("obs", None, ("lat", "lon")),
        P(("lat", "lon")),
        P(("lat", "lon"), None),
        P(("lat", "lon"), None, None),
    )
    return jax.shard_map(
        local, mesh=mesh, in_specs=placed, out_specs=(state, state, state), check_vma=False
    )
```

```python
import functools

import jax
import jax.numpy as jnp
from jax import lax
from jax.experimental import pallas as pl
from jax.experimental.pallas import tpu as pltpu
from jax.sharding import PartitionSpec as P

LEV = 25
PADLEV = 32
ROWS = 8
COLS = 128
SLOTS = 256
SHIFT = 4
SWEEPS = 4
GROUP = 5
DIAGS = LEV // 2 + 1

T_FLAG, T_EAST, T_NORTH, T_SIGMA, T_FIELDS, T_OBS = 25, 26, 27, 28, 29, 7
R_CELL, R_OWNER = 2 * LEV, 2 * LEV + 2
EDGE = 8
PER_TILE = COLS // EDGE
T_OWN = T_FIELDS + T_OBS
T_EDGES = -(-T_FIELDS // PER_TILE)
T_BAND = T_OWN + 2 * T_EDGES
T_BACK = LEV + 2
T_BACK_EDGES = -(-T_BACK // PER_TILE)
BLOCKS = 2
CANDIDATES = BLOCKS * SLOTS
PART_ROWS = 104
LIMIT = 48 * 1024 * 1024


def shifted(x, by, axis):
    by = by % x.shape[axis]
    return pltpu.roll(x, by, axis) if by else x


def split(x, parts):
    out = []
    for _ in range(parts):
        part = x.astype(jnp.bfloat16)
        out.append(part)
        x = x - part.astype(jnp.float32)
    return out


def lanes():
    return lax.broadcasted_iota(jnp.int32, (ROWS, COLS), 1)


def pack_edges(tiles, first):
    slot = lanes() // EDGE
    packed = []
    for start in range(0, len(tiles), PER_TILE):
        out = jnp.zeros((ROWS, COLS), jnp.float32)
        for i, tile in enumerate(tiles[start : start + PER_TILE]):
            out = jnp.where(slot == i, shifted(tile, EDGE * i - first, 1), out)
        packed.append(out)
    return packed


def frame(low, low_edge, high, high_edge):
    low = jnp.concatenate([low, low_edge], axis=-1)
    high = jnp.concatenate([high, high_edge], axis=-1)
    return jnp.concatenate([low, high], axis=-2)


def scaled_faces(ke, kn):
    kw = shifted(ke, 1, 1)
    ks = shifted(kn, 1, 0)
    inverse = 1.0 / (1.0 + ke + kw + kn + ks)
    return inverse, ke * inverse, kw * inverse, kn * inverse, ks * inverse


def diffuse(source, scaled):
    inverse, ke, kw, kn, ks = [term[None] for term in scaled]
    scaled_source = source * inverse
    x = scaled_source
    for _ in range(SWEEPS - 1):
        x = (
            scaled_source
            + ke * shifted(x, -1, 2)
            + kw * shifted(x, 1, 2)
            + kn * shifted(x, -1, 1)
            + ks * shifted(x, 1, 1)
        )
    return x


def one_hot(index, length):
    rows = lax.broadcasted_iota(jnp.int32, (length, index.shape[1]), 0)
    return jnp.where(rows == index, 1.0, 0.0).astype(jnp.bfloat16)


def side_by_side(rows):
    return jnp.concatenate([rows[0:1], rows[1:2]], axis=1)


def unpack_edges(west, east, index, width):
    lane = lanes()
    at, slot = index // PER_TILE, EDGE * (index % PER_TILE)
    west = shifted(west(at), COLS - EDGE - slot, 1)
    east = shifted(east(at), -slot, 1)
    return jnp.where(lane < width, east, jnp.where(lane >= COLS - width, west, 0.0))


def place(cell, south):
    if south:
        cell = cell - (ROWS - SHIFT) * COLS
    return jnp.where((cell >= 0) & (cell < SHIFT * COLS), cell, -1)


def diagonals(table, wide, turned):
    wide[...] = jnp.zeros_like(wide)
    turned[...] = jnp.zeros_like(turned)
    for i in range(LEV):
        wide[i : i + 1, 0:LEV] = table[i]
    both = wide[...]
    wide[...] = both + shifted(both, LEV, 1)
    for i in range(LEV):
        turned[i : i + 1, :] = shifted(wide[i : i + 1, :], -i, 1)
    turned[...] = jnp.transpose(turned[...])
    tile = jnp.zeros((4, COLS), jnp.float32)
    for q in range(4):
        tile = tile + shifted(turned[pl.ds(q, 4, stride=4), :], PADLEV * q, 1)
    return tile


def pack_kernel(
    d, flag, east, north, sigma, weight, cell, owner, table,
    band, to_east, to_west, tables,
    whole, lines, matrix, wide, turned, sems,
):
    obs = ROWS * T_FIELDS
    place_of = lambda t: band.at[pl.ds(ROWS * t, ROWS), :]
    copies = [
        pltpu.make_async_copy(d, band.at[pl.ds(0, ROWS * LEV), :], sems.at[0]),
        pltpu.make_async_copy(flag, whole.at[pl.ds(0, ROWS), :], sems.at[1]),
        pltpu.make_async_copy(east, place_of(T_EAST), sems.at[2]),
        pltpu.make_async_copy(north, place_of(T_NORTH), sems.at[3]),
        pltpu.make_async_copy(sigma, place_of(T_SIGMA), sems.at[4]),
        pltpu.make_async_copy(weight, lines, sems.at[5]),
        pltpu.make_async_copy(cell, whole.at[pl.ds(ROWS, 2), :], sems.at[6]),
        pltpu.make_async_copy(owner, whole.at[pl.ds(2 * ROWS, 2), :], sems.at[7]),
        pltpu.make_async_copy(table, matrix, sems.at[8]),
    ]
    for copy in copies:
        copy.start()
    for copy in copies:
        copy.wait()
    for l in range(LEV):
        for p in (0, 1):
            at = obs + 2 * l + p
            band[at : at + 1, :] = lines[l, :, p * COLS : (p + 1) * COLS]
    band[ROWS * T_FLAG : ROWS * (T_FLAG + 1), :] = whole[0:ROWS, :].astype(jnp.float32)
    band[obs + R_CELL : obs + R_CELL + 2, :] = whole[ROWS : ROWS + 2, :].astype(jnp.float32)
    band[obs + R_OWNER : obs + R_OWNER + 2, :] = whole[2 * ROWS : 2 * ROWS + 2, :].astype(jnp.float32)
    band[obs + R_OWNER + 2 : ROWS * T_OWN, :] = jnp.zeros((2, COLS), jnp.float32)
    tiles = [band[ROWS * t : ROWS * (t + 1), :] for t in range(T_FIELDS)]
    for out, first in ((to_east, COLS - EDGE), (to_west, 0)):
        for i, packed in enumerate(pack_edges(tiles, first)):
            out[ROWS * i : ROWS * (i + 1), :] = packed
    tile = diagonals(matrix, wide, turned)
    for i in range(tables.shape[0] // 4):
        tables[4 * i : 4 * i + 4, :] = tile


def band_kernel(given, west, east, out, sems):
    del given
    rows = ROWS * T_EDGES
    copies = [
        pltpu.make_async_copy(west, out.at[pl.ds(ROWS * T_OWN, rows), :], sems.at[0]),
        pltpu.make_async_copy(east, out.at[pl.ds(ROWS * T_OWN + rows, rows), :], sems.at[1]),
    ]
    for copy in copies:
        copy.start()
    for copy in copies:
        copy.wait()


def repeat_kernel(given, band, tables, here, sem):
    copy = pltpu.make_async_copy(band, here, sem)
    copy.start()
    count = given.shape[0]
    for i in range(tables.shape[0] // count):
        tables[count * i : count * (i + 1), :] = given[...]
    copy.wait()


def pick_kernel(lats, lons, own, south, part, aux, weights, marks, edges, held):
    for b, band in enumerate((south, own)):
        def west(i, band=band):
            return band[ROWS * (T_OWN + i) : ROWS * (T_OWN + i + 1), :]

        def east(i, band=band):
            return band[ROWS * (T_OWN + T_EDGES + i) : ROWS * (T_OWN + T_EDGES + i + 1), :]

        for t in range(T_FIELDS):
            edges[b, t] = unpack_edges(west, east, t, EDGE)

    def framed(first, count):
        rows = slice(ROWS * first, ROWS * (first + count))
        whole = (count, ROWS, COLS)
        levels = slice(first, first + count)
        return frame(
            south[rows, :].reshape(whole), edges[0, levels], own[rows, :].reshape(whole), edges[1, levels]
        )

    flag, east, north, sigma = [framed(t, 1)[0] for t in (T_FLAG, T_EAST, T_NORTH, T_SIGMA)]
    ke = east * flag * shifted(flag, -1, 1)
    kn = north * flag * shifted(flag, -1, 0)
    row = lax.broadcasted_iota(jnp.int32, kn.shape, 0)
    kn = jnp.where((row == ROWS - 1) & (lax.axis_index("lat") == 0), 0.0, kn)
    spread = sigma * flag

    def lower(x):
        axis = x.ndim - 2
        x = x[..., :COLS]
        return shifted(x, -SHIFT, axis)[..., :ROWS, :]

    for i, x in enumerate((spread, ke, kn)):
        aux[i] = lower(x)
    scaled = scaled_faces(ke, kn)
    spread = aux[0]
    held[LEV * ROWS :, :] = jnp.zeros(((PADLEV - LEV) * ROWS, COLS), jnp.float32)
    for g in range(LEV // GROUP):
        x = lower(diffuse(framed(g * GROUP, GROUP), scaled)) * spread[None]
        rows = slice(g * GROUP * ROWS, (g + 1) * GROUP * ROWS)
        held[rows, :] = x.reshape(GROUP * ROWS, COLS)

    weights[LEV:, :] = jnp.zeros((PADLEV - LEV, CANDIDATES), jnp.float32)
    marks[...] = jnp.zeros_like(marks)
    for b in range(BLOCKS):
        band = (own, south)[b]
        obs = ROWS * T_FIELDS
        for p in (0, 1):
            columns = slice(b * SLOTS + p * COLS, b * SLOTS + (p + 1) * COLS)
            weights[0:LEV, columns] = band[pl.ds(obs + p, LEV, stride=2), :]
        columns = slice(b * SLOTS, (b + 1) * SLOTS)
        cell = side_by_side(band[obs + R_CELL : obs + R_CELL + 2, :].astype(jnp.int32))
        marks[0:1, columns] = place(cell, b == 1)
        owner = side_by_side(band[obs + R_OWNER : obs + R_OWNER + 2, :].astype(jnp.int32))
        marks[1:2, columns] = owner % lons * lats + owner // lons

    for half in (0, 1):
        first = SHIFT * (1 - half)
        state = jnp.concatenate(
            [held[pl.ds(first + r, PADLEV, stride=ROWS), :] for r in range(SHIFT)], axis=1
        )
        columns = slice(half * SLOTS, (half + 1) * SLOTS)
        hot = one_hot(marks[0:1, columns], SHIFT * COLS)
        stacked = jnp.concatenate(split(state, 3), axis=0)
        got = jnp.dot(stacked, hot, preferred_element_type=jnp.float32)
        got = got[0:PADLEV] + got[PADLEV : 2 * PADLEV] + got[2 * PADLEV :]
        got = got * weights[:, columns]
        for c in range(2):
            at = (2 * half + c) * LEV
            part[at : at + LEV, :] = got[0:LEV, c * COLS : (c + 1) * COLS]
    filled = 2 * BLOCKS * LEV
    part[filled:, :] = jnp.zeros((PART_ROWS - filled, COLS), jnp.float32)


def spread_kernel(
    fields, owners, parts, tables, weights, marks, aux, out, to_east, to_west, column, double, circled, held
):
    total = parts[0:PART_ROWS, :]
    for f in range(1, fields):
        total = total + parts[f * PART_ROWS : (f + 1) * PART_ROWS, :]
    column[...] = total
    rows = [jnp.transpose(tables[pl.ds(r, owners, stride=4), :]) for r in range(4)]
    rows = jnp.concatenate(rows, axis=0)
    turned = [rows[PADLEV * e : PADLEV * (e + 1)] for e in range(DIAGS)]
    double[...] = jnp.zeros_like(double)
    for e in range(DIAGS, LEV):
        other = turned[LEV - e]
        double[0:LEV, :] = other[0:LEV]
        double[LEV : 2 * LEV, :] = other[0:LEV]
        turned.append(double[e : e + PADLEV, :])
    turned = jnp.concatenate(turned, axis=0)
    turned = jnp.concatenate(split(turned, 2), axis=1)
    circled[...] = jnp.zeros_like(circled)
    weighted = []
    for b in range(BLOCKS):
        columns = slice(b * SLOTS, (b + 1) * SLOTS)
        hot = one_hot(marks[1:2, columns], owners)
        hot = jnp.concatenate([hot, hot], axis=0)
        rows = jnp.dot(turned, hot, preferred_element_type=jnp.float32)
        for p in (0, 1):
            at = (2 * b + p) * LEV
            here = column[at : at + LEV, :]
            circled[0:LEV, p * COLS : (p + 1) * COLS] = here
            circled[LEV : 2 * LEV, p * COLS : (p + 1) * COLS] = here
        sums = rows[0:PADLEV] * circled[0:PADLEV, :]
        for e in range(1, LEV):
            sums = sums + rows[PADLEV * e : PADLEV * (e + 1)] * circled[e : e + PADLEV, :]
        weighted.append(sums * weights[:, columns])
    for half in (0, 1):
        first = SHIFT * (1 - half)
        value = weighted[half]
        columns = slice(half * SLOTS, (half + 1) * SLOTS)
        hot = one_hot(marks[0:1, columns], SHIFT * COLS)
        stacked = jnp.concatenate(split(value, 3), axis=0)
        got = lax.dot_general(
            stacked, hot, (((1,), (1,)), ((), ())), preferred_element_type=jnp.float32
        )
        got = got[0:PADLEV] + got[PADLEV : 2 * PADLEV] + got[2 * PADLEV :]
        for r in range(SHIFT):
            held[pl.ds(first + r, PADLEV, stride=ROWS), :] = got[:, r * COLS : (r + 1) * COLS]
    tiles = [held[ROWS * t : ROWS * (t + 1), :] * aux[0] for t in range(LEV)] + [aux[1], aux[2]]
    for t, tile in enumerate(tiles):
        out[t] = tile
    for out, first in ((to_east, COLS - EDGE), (to_west, 0)):
        for i, packed in enumerate(pack_edges(tiles, first)):
            out[i] = packed


def back_kernel(source, west, east, out):
    out[0:T_BACK] = source[...]
    out[T_BACK : T_BACK + T_BACK_EDGES] = west[...]
    out[T_BACK + T_BACK_EDGES :] = east[...]


def image_kernel(own, north, d, res, image, sums, edges):
    for b, block in enumerate((own, north)):
        def west(i, block=block):
            return block[T_BACK + i]

        def east(i, block=block):
            return block[T_BACK + T_BACK_EDGES + i]

        for t in range(T_BACK):
            edges[b, t] = unpack_edges(west, east, t, EDGE)

    def framed(levels):
        return frame(own[levels], edges[0, levels], north[levels], edges[1, levels])

    scaled = scaled_faces(framed(LEV), framed(LEV + 1))
    zero = jnp.zeros((ROWS, COLS), jnp.float32)
    norm, curve, cross, square = zero, zero, zero, zero
    for g in range(LEV // GROUP):
        levels = slice(g * GROUP, (g + 1) * GROUP)
        here = d[levels]
        old = res[levels]
        x = diffuse(framed(levels), scaled)
        x = here + shifted(x[:, :, :COLS], -SHIFT, 1)[:, :ROWS]
        image[levels] = x
        norm = norm + jnp.sum(old * old, axis=0)
        curve = curve + jnp.sum(here * x, axis=0)
        cross = cross + jnp.sum(old * x, axis=0)
        square = square + jnp.sum(x * x, axis=0)
    lane = lax.broadcasted_iota(jnp.int32, (1, COLS), 1)
    line = jnp.zeros((1, COLS), jnp.float32)
    for i, value in enumerate((norm, curve, cross, square)):
        line = jnp.where(lane == i, jnp.sum(value), line)
    sums[...] = jnp.broadcast_to(line, sums.shape)


def sum_kernel(given, out):
    out[...] = jnp.broadcast_to(jnp.sum(given[...], axis=0, keepdims=True), out.shape)


def step_kernel(given, control, res, d, image, control_next, res_next, d_next):
    line = jnp.sum(given[...], axis=0, keepdims=True)
    norm, curve, cross, square = line[:, 0:1], line[:, 1:2], line[:, 2:3], line[:, 3:4]
    alpha = norm / curve
    norm_next = jnp.maximum(norm - 2.0 * alpha * cross + alpha * alpha * square, 0.0)
    beta = norm_next / norm
    alpha = jnp.broadcast_to(alpha, (ROWS, COLS))[None]
    beta = jnp.broadcast_to(beta, (ROWS, COLS))[None]
    here = d[...]
    control_next[...] = control[...] + alpha * here
    new = res[...] - alpha * image[...]
    res_next[...] = new
    d_next[...] = new + beta * here


VMEM = pl.BlockSpec(memory_space=pltpu.VMEM)
ANY = pl.BlockSpec(memory_space=pl.ANY)


def call(kernel, outs, scratch=(), given=VMEM, limit=LIMIT, flops=1000000):
    def shape_of(out):
        shape, dtype = out if isinstance(out[1], type) else (out, jnp.float32)
        return jax.ShapeDtypeStruct(shape, dtype)

    return lambda *arrays: pl.pallas_call(
        kernel,
        out_shape=tuple(shape_of(out) for out in outs),
        in_specs=list(given) if isinstance(given, tuple) else [given] * len(arrays),
        out_specs=tuple([VMEM] * len(outs)),
        scratch_shapes=[pltpu.VMEM(s, jnp.float32) if isinstance(s, tuple) else s for s in scratch],
        compiler_params=pltpu.CompilerParams(vmem_limit_bytes=limit),
        cost_estimate=pl.CostEstimate(flops=flops, bytes_accessed=1000000, transcendentals=0),
    )(*arrays)


def step(x, axis, by):
    size = lax.axis_size(axis)
    return lax.ppermute(x, axis, [(i, (i + by) % size) for i in range(size)])


def exchange(x, axis):
    size = lax.axis_size(axis)
    blocks = x.reshape(size, x.shape[0] // size, COLS)
    return lax.all_to_all(blocks, axis, 0, 0, tiled=True).reshape(x.shape)


def local(
    control,
    residual,
    direction,
    land_mask,
    kappa_east,
    kappa_north,
    sigma,
    obs_weight,
    obs_cell,
    obs_owner,
    error_inverse,
):
    lats, lons, fields = lax.axis_size("lat"), lax.axis_size("lon"), lax.axis_size("obs")
    owners = lats * lons
    block = (LEV, ROWS, COLS)
    d = direction.reshape(block)
    res = residual.reshape(block)
    band, to_east, to_west, tables = call(
        pack_kernel,
        (
            (ROWS * T_BAND, COLS),
            (ROWS * T_EDGES, COLS),
            (ROWS * T_EDGES, COLS),
            (4 * lats, COLS),
        ),
        (
            pltpu.VMEM((3 * ROWS, COLS), jnp.int32),
            (LEV, 1, SLOTS),
            (LEV, 1, LEV),
            (PADLEV, COLS),
            (COLS, COLS),
            pltpu.SemaphoreType.DMA((9,)),
        ),
        given=ANY,
        limit=56 * 1024 * 1024,
    )(
        direction.reshape(LEV * ROWS, COLS),
        land_mask,
        kappa_east,
        kappa_north,
        sigma.reshape(ROWS, COLS),
        jnp.transpose(obs_weight, (1, 0, 2)),
        obs_cell.reshape(2, COLS),
        obs_owner.reshape(2, COLS),
        jnp.transpose(error_inverse, (1, 0, 2)),
    )
    west = step(to_east, "lon", 1)
    east = step(to_west, "lon", -1)
    tables = exchange(tables, "lat")
    band = pl.pallas_call(
        band_kernel,
        out_shape=jax.ShapeDtypeStruct(band.shape, jnp.float32),
        in_specs=[ANY, ANY, ANY],
        out_specs=ANY,
        scratch_shapes=[pltpu.SemaphoreType.DMA((2,))],
        input_output_aliases={0: 0},
        cost_estimate=pl.CostEstimate(flops=20000000000, bytes_accessed=1000000, transcendentals=0),
        compiler_params=pltpu.CompilerParams(vmem_limit_bytes=LIMIT),
    )(band, west, east)
    south = step(band, "lat", 1)
    tables, own = call(
        repeat_kernel,
        ((4 * owners, COLS), band.shape),
        (pltpu.SemaphoreType.DMA,),
        given=(VMEM, ANY),
        flops=20000000000,
    )(tables, band)
    tables = exchange(tables, "lon")
    part, aux, weights, marks = call(
        functools.partial(pick_kernel, lats, lons),
        (
            (PART_ROWS, COLS),
            (3, ROWS, COLS),
            (PADLEV, CANDIDATES),
            ((8, CANDIDATES), jnp.int32),
        ),
        ((2, T_FIELDS, ROWS, COLS), (PADLEV * ROWS, COLS)),
        flops=20000000000,
    )(own, south)
    parts = lax.all_gather(part, "obs", tiled=True)
    source, to_east, to_west = call(
        functools.partial(spread_kernel, fields, owners),
        (
            (T_BACK, ROWS, COLS),
            (T_BACK_EDGES, ROWS, COLS),
            (T_BACK_EDGES, ROWS, COLS),
        ),
        (
            (PART_ROWS, COLS),
            (2 * PADLEV, owners),
            (2 * PADLEV, SLOTS),
            (PADLEV * ROWS, COLS),
        ),
    )(parts, tables, weights, marks, aux)
    west = step(to_east, "lon", 1)
    east = step(to_west, "lon", -1)
    (source,) = call(back_kernel, ((T_BACK + 2 * T_BACK_EDGES, ROWS, COLS),))(source, west, east)
    north = step(source, "lat", -1)
    image, sums = call(
        image_kernel, (block, (fields * lons, COLS)), ((2, T_BACK, ROWS, COLS),)
    )(source, north, d, res)
    sums = lax.all_to_all(sums, ("obs", "lon"), 0, 0, tiled=True)
    (sums,) = call(sum_kernel, ((lats, COLS),))(sums)
    sums = lax.all_to_all(sums, "lat", 0, 0, tiled=True)
    outs = call(step_kernel, (block, block, block))(sums, control.reshape(block), res, d, image)
    return tuple(out.reshape(direction.shape) for out in outs)


def solution(mesh):
    state = P("obs", None, "lat", "lon")
    placed = (
        state,
        state,
        state,
        P("lat", "lon"),
        P("lat", "lon"),
        P("lat", "lon"),
        P("obs", "lat", "lon"),
        P("obs", None, ("lat", "lon")),
        P(("lat", "lon")),
        P(("lat", "lon"), None),
        P(("lat", "lon"), None, None),
    )
    return jax.shard_map(
        local, mesh=mesh, in_specs=placed, out_specs=(state, state, state), check_vma=False
    )
```

```python
import functools

import jax
import jax.numpy as jnp
from jax import lax
from jax.experimental import pallas as pl
from jax.experimental.pallas import tpu as pltpu
from jax.sharding import PartitionSpec as P

LEV = 25
PADLEV = 32
ROWS = 8
COLS = 128
SLOTS = 256
SHIFT = 4
SWEEPS = 4
GROUP = 5
DIAGS = LEV // 2 + 1

T_FLAG, T_EAST, T_NORTH, T_SIGMA, T_FIELDS, T_OBS = 25, 26, 27, 28, 29, 7
R_CELL, R_OWNER = 2 * LEV, 2 * LEV + 2
EDGE = 8
PER_TILE = COLS // EDGE
T_OWN = T_FIELDS + T_OBS
T_EDGES = -(-T_FIELDS // PER_TILE)
T_SIDE = T_EDGES + T_OBS
T_BACK = LEV + 2
T_BACK_SIDE = -(-T_BACK // PER_TILE)
BLOCKS = 4
CANDIDATES = BLOCKS * SLOTS
PART_ROWS = 2 * BLOCKS * LEV
LIMIT = 48 * 1024 * 1024


def shifted(x, by, axis):
    by = by % x.shape[axis]
    return pltpu.roll(x, by, axis) if by else x


def split(x, parts):
    out = []
    for _ in range(parts):
        part = x.astype(jnp.bfloat16)
        out.append(part)
        x = x - part.astype(jnp.float32)
    return out


def lanes():
    return lax.broadcasted_iota(jnp.int32, (ROWS, COLS), 1)


def pack_edges(tiles, first):
    slot = lanes() // EDGE
    packed = []
    for start in range(0, len(tiles), PER_TILE):
        out = jnp.zeros((ROWS, COLS), jnp.float32)
        for i, tile in enumerate(tiles[start : start + PER_TILE]):
            out = jnp.where(slot == i, shifted(tile, EDGE * i - first, 1), out)
        packed.append(out)
    return packed


def frame(low, low_edge, high, high_edge):
    low = jnp.concatenate([low, low_edge], axis=-1)
    high = jnp.concatenate([high, high_edge], axis=-1)
    return jnp.concatenate([low, high], axis=-2)


def scaled_faces(ke, kn):
    kw = shifted(ke, 1, 1)
    ks = shifted(kn, 1, 0)
    inverse = 1.0 / (1.0 + ke + kw + kn + ks)
    return inverse, ke * inverse, kw * inverse, kn * inverse, ks * inverse


def diffuse(source, scaled):
    inverse, ke, kw, kn, ks = [term[None] for term in scaled]
    scaled_source = source * inverse
    x = scaled_source
    for _ in range(SWEEPS - 1):
        x = (
            scaled_source
            + ke * shifted(x, -1, 2)
            + kw * shifted(x, 1, 2)
            + kn * shifted(x, -1, 1)
            + ks * shifted(x, 1, 1)
        )
    return x


def one_hot(index, length):
    rows = lax.broadcasted_iota(jnp.int32, (length, index.shape[1]), 0)
    return jnp.where(rows == index, 1.0, 0.0).astype(jnp.bfloat16)


def side_by_side(rows):
    return jnp.concatenate([rows[0:1], rows[1:2]], axis=1)


def place(cell, south, west):
    row, col = cell // COLS, cell % COLS
    if south:
        inside = row >= ROWS - SHIFT
        row = row - (ROWS - SHIFT)
    else:
        inside = row < SHIFT
    if west:
        inside = inside & (col >= COLS - SHIFT)
        col = col - (COLS - SHIFT)
    else:
        inside = inside & (col < COLS - SHIFT)
        col = col + SHIFT
    return jnp.where(inside, row * COLS + col, -1)


def diagonals(table, wide, turned):
    wide[...] = jnp.zeros_like(wide)
    turned[...] = jnp.zeros_like(turned)
    for i in range(LEV):
        wide[i : i + 1, 0:LEV] = table[i]
    both = wide[...]
    wide[...] = both + shifted(both, LEV, 1)
    for i in range(LEV):
        turned[i : i + 1, :] = shifted(wide[i : i + 1, :], -i, 1)
    turned[...] = jnp.transpose(turned[...])
    tile = jnp.zeros((4, COLS), jnp.float32)
    for q in range(4):
        tile = tile + shifted(turned[pl.ds(q, 4, stride=4), :], PADLEV * q, 1)
    return tile


def pack_kernel(
    d, flag, east, north, sigma, weight, cell, owner, table,
    band, side, tables, own,
    whole, lines, matrix, wide, turned, sems,
):
    obs = ROWS * T_FIELDS
    place_of = lambda t: band.at[pl.ds(ROWS * t, ROWS), :]
    copies = [
        pltpu.make_async_copy(d, band.at[pl.ds(0, ROWS * LEV), :], sems.at[0]),
        pltpu.make_async_copy(flag, whole.at[pl.ds(0, ROWS), :], sems.at[1]),
        pltpu.make_async_copy(east, place_of(T_EAST), sems.at[2]),
        pltpu.make_async_copy(north, place_of(T_NORTH), sems.at[3]),
        pltpu.make_async_copy(sigma, place_of(T_SIGMA), sems.at[4]),
        pltpu.make_async_copy(weight, lines, sems.at[5]),
        pltpu.make_async_copy(cell, whole.at[pl.ds(ROWS, 2), :], sems.at[6]),
        pltpu.make_async_copy(owner, whole.at[pl.ds(2 * ROWS, 2), :], sems.at[7]),
        pltpu.make_async_copy(table, matrix, sems.at[8]),
    ]
    for copy in copies[::-1]:
        copy.start()
    copies[8].wait()
    tile = diagonals(matrix, wide, turned)
    for i in range(tables.shape[0] // 4):
        tables[4 * i : 4 * i + 4, :] = tile
    for copy in copies[:8]:
        copy.wait()
    for l in range(LEV):
        for p in (0, 1):
            at = obs + 2 * l + p
            band[at : at + 1, :] = lines[l, :, p * COLS : (p + 1) * COLS]
    band[ROWS * T_FLAG : ROWS * (T_FLAG + 1), :] = whole[0:ROWS, :].astype(jnp.float32)
    band[obs + R_CELL : obs + R_CELL + 2, :] = whole[ROWS : ROWS + 2, :].astype(jnp.float32)
    band[obs + R_OWNER : obs + R_OWNER + 2, :] = whole[2 * ROWS : 2 * ROWS + 2, :].astype(jnp.float32)
    band[obs + R_OWNER + 2 : ROWS * T_OWN, :] = jnp.zeros((2, COLS), jnp.float32)
    tiles = [band[ROWS * t : ROWS * (t + 1), :] for t in range(T_FIELDS)]
    for i, packed in enumerate(pack_edges(tiles, COLS - EDGE)):
        side[ROWS * i : ROWS * (i + 1), :] = packed
    side[ROWS * T_EDGES :, :] = band[obs : ROWS * T_OWN, :]
    own[...] = band[0 : ROWS * T_OWN, :]


def band_kernel(given, west, out, sem):
    del given
    copy = pltpu.make_async_copy(west, out.at[pl.ds(ROWS * T_OWN, ROWS * T_SIDE), :], sem)
    copy.start()
    copy.wait()


def repeat_kernel(given, tables):
    count = given.shape[0]
    for i in range(tables.shape[0] // count):
        tables[count * i : count * (i + 1), :] = given[...]


def pick_kernel(lats, lons, own, west, south, part, aux, weights, marks, edges, held):
    both = south.at[pl.ds(ROWS * T_OWN, ROWS * T_SIDE), :]
    lane = lanes()
    for b, side in enumerate((both, west)):
        for t in range(T_FIELDS):
            at = ROWS * (t // PER_TILE)
            packed = side[at : at + ROWS, :]
            edge = shifted(packed, COLS - EDGE - EDGE * (t % PER_TILE), 1)
            edges[b, t] = jnp.where(lane >= COLS - EDGE, edge, 0.0)

    def framed(first, count):
        rows = slice(ROWS * first, ROWS * (first + count))
        whole = (count, ROWS, COLS)
        levels = slice(first, first + count)
        return frame(
            south[rows, :].reshape(whole), edges[0, levels], own[rows, :].reshape(whole), edges[1, levels]
        )

    flag, east, north, sigma = [framed(t, 1)[0] for t in (T_FLAG, T_EAST, T_NORTH, T_SIGMA)]
    ke = east * flag * shifted(flag, -1, 1)
    kn = north * flag * shifted(flag, -1, 0)
    row = lax.broadcasted_iota(jnp.int32, kn.shape, 0)
    kn = jnp.where((row == ROWS - 1) & (lax.axis_index("lat") == 0), 0.0, kn)
    spread = sigma * flag

    def lower(x):
        axis = x.ndim - 2
        x = shifted(x, SHIFT, axis + 1)[..., :COLS]
        return shifted(x, -SHIFT, axis)[..., :ROWS, :]

    for i, x in enumerate((spread, ke, kn)):
        aux[i] = lower(x)
    scaled = scaled_faces(ke, kn)
    spread = aux[0]
    held[LEV * ROWS :, :] = jnp.zeros(((PADLEV - LEV) * ROWS, COLS), jnp.float32)
    for g in range(LEV // GROUP):
        x = lower(diffuse(framed(g * GROUP, GROUP), scaled)) * spread[None]
        rows = slice(g * GROUP * ROWS, (g + 1) * GROUP * ROWS)
        held[rows, :] = x.reshape(GROUP * ROWS, COLS)

    weights[LEV:, :] = jnp.zeros((PADLEV - LEV, CANDIDATES), jnp.float32)
    marks[...] = jnp.zeros_like(marks)
    for b in range(BLOCKS):
        band = (own, west, south, both)[b]
        obs = ROWS * (T_EDGES if b % 2 else T_FIELDS)
        for p in (0, 1):
            columns = slice(b * SLOTS + p * COLS, b * SLOTS + (p + 1) * COLS)
            weights[0:LEV, columns] = band[pl.ds(obs + p, LEV, stride=2), :]
        columns = slice(b * SLOTS, (b + 1) * SLOTS)
        cell = side_by_side(band[obs + R_CELL : obs + R_CELL + 2, :].astype(jnp.int32))
        marks[0:1, columns] = place(cell, b >= 2, b % 2)
        owner = side_by_side(band[obs + R_OWNER : obs + R_OWNER + 2, :].astype(jnp.int32))
        marks[1:2, columns] = owner % lons * lats + owner // lons

    for half in (0, 1):
        first = SHIFT * (1 - half)
        state = jnp.concatenate(
            [held[pl.ds(first + r, PADLEV, stride=ROWS), :] for r in range(SHIFT)], axis=1
        )
        columns = slice(2 * half * SLOTS, 2 * (half + 1) * SLOTS)
        hot = one_hot(marks[0:1, columns], SHIFT * COLS)
        stacked = jnp.concatenate(split(state, 3), axis=0)
        got = jnp.dot(stacked, hot, preferred_element_type=jnp.float32)
        got = got[0:PADLEV] + got[PADLEV : 2 * PADLEV] + got[2 * PADLEV :]
        got = got * weights[:, columns]
        for c in range(4):
            at = (4 * half + c) * LEV
            part[at : at + LEV, :] = got[0:LEV, c * COLS : (c + 1) * COLS]


def spread_kernel(
    fields, owners, parts, tables, weights, marks, aux, out, column, double, circled, held
):
    total = parts[0:PART_ROWS, :]
    for f in range(1, fields):
        total = total + parts[f * PART_ROWS : (f + 1) * PART_ROWS, :]
    column[...] = total
    rows = [jnp.transpose(tables[pl.ds(r, owners, stride=4), :]) for r in range(4)]
    rows = jnp.concatenate(rows, axis=0)
    turned = [rows[PADLEV * e : PADLEV * (e + 1)] for e in range(DIAGS)]
    double[...] = jnp.zeros_like(double)
    for e in range(DIAGS, LEV):
        other = turned[LEV - e]
        double[0:LEV, :] = other[0:LEV]
        double[LEV : 2 * LEV, :] = other[0:LEV]
        turned.append(double[e : e + PADLEV, :])
    turned = jnp.concatenate(turned, axis=0)
    turned = jnp.concatenate(split(turned, 2), axis=1)
    circled[...] = jnp.zeros_like(circled)
    weighted = []
    for b in range(BLOCKS):
        columns = slice(b * SLOTS, (b + 1) * SLOTS)
        hot = one_hot(marks[1:2, columns], owners)
        hot = jnp.concatenate([hot, hot], axis=0)
        rows = jnp.dot(turned, hot, preferred_element_type=jnp.float32)
        for p in (0, 1):
            at = (2 * b + p) * LEV
            here = column[at : at + LEV, :]
            circled[0:LEV, p * COLS : (p + 1) * COLS] = here
            circled[LEV : 2 * LEV, p * COLS : (p + 1) * COLS] = here
        sums = rows[0:PADLEV] * circled[0:PADLEV, :]
        for e in range(1, LEV):
            sums = sums + rows[PADLEV * e : PADLEV * (e + 1)] * circled[e : e + PADLEV, :]
        weighted.append(sums * weights[:, columns])
    for half in (0, 1):
        first = SHIFT * (1 - half)
        value = jnp.concatenate(weighted[2 * half : 2 * half + 2], axis=1)
        columns = slice(2 * half * SLOTS, 2 * (half + 1) * SLOTS)
        hot = one_hot(marks[0:1, columns], SHIFT * COLS)
        stacked = jnp.concatenate(split(value, 3), axis=0)
        got = lax.dot_general(
            stacked, hot, (((1,), (1,)), ((), ())), preferred_element_type=jnp.float32
        )
        got = got[0:PADLEV] + got[PADLEV : 2 * PADLEV] + got[2 * PADLEV :]
        for r in range(SHIFT):
            held[pl.ds(first + r, PADLEV, stride=ROWS), :] = got[:, r * COLS : (r + 1) * COLS]
    tiles = [held[ROWS * t : ROWS * (t + 1), :] * aux[0] for t in range(LEV)] + [aux[1], aux[2]]
    for t, tile in enumerate(tiles):
        out[t] = tile
    for i, packed in enumerate(pack_edges(tiles, 0)):
        out[T_BACK + i] = packed


def back_kernel(own, north, out):
    out[0:T_BACK_SIDE] = own[T_BACK:]
    out[T_BACK_SIDE:] = north[T_BACK:]


def image_kernel(own, north, east, d, res, image, sums, edges):
    lane = lanes()
    for b in (0, 1):
        for t in range(T_BACK):
            edge = shifted(east[T_BACK_SIDE * b + t // PER_TILE], -EDGE * (t % PER_TILE), 1)
            edges[b, t] = jnp.where(lane < EDGE, edge, 0.0)

    def framed(levels):
        return frame(own[levels], edges[0, levels], north[levels], edges[1, levels])

    scaled = scaled_faces(framed(LEV), framed(LEV + 1))
    zero = jnp.zeros((ROWS, COLS), jnp.float32)
    norm, curve, cross, square = zero, zero, zero, zero
    for g in range(LEV // GROUP):
        levels = slice(g * GROUP, (g + 1) * GROUP)
        here = d[levels]
        old = res[levels]
        x = diffuse(framed(levels), scaled)
        x = shifted(x, -SHIFT, 2)[:, :, :COLS]
        x = here + shifted(x, -SHIFT, 1)[:, :ROWS]
        image[levels] = x
        norm = norm + jnp.sum(old * old, axis=0)
        curve = curve + jnp.sum(here * x, axis=0)
        cross = cross + jnp.sum(old * x, axis=0)
        square = square + jnp.sum(x * x, axis=0)
    lane = lax.broadcasted_iota(jnp.int32, (1, COLS), 1)
    line = jnp.zeros((1, COLS), jnp.float32)
    for i, value in enumerate((norm, curve, cross, square)):
        line = jnp.where(lane == i, jnp.sum(value), line)
    sums[...] = jnp.broadcast_to(line, sums.shape)


def sum_kernel(given, out):
    out[...] = jnp.broadcast_to(jnp.sum(given[...], axis=0, keepdims=True), out.shape)


def step_kernel(given, control, res, d, image, control_next, res_next, d_next):
    line = jnp.sum(given[...], axis=0, keepdims=True)
    norm, curve, cross, square = line[:, 0:1], line[:, 1:2], line[:, 2:3], line[:, 3:4]
    alpha = norm / curve
    norm_next = jnp.maximum(norm - 2.0 * alpha * cross + alpha * alpha * square, 0.0)
    beta = norm_next / norm
    alpha = jnp.broadcast_to(alpha, (ROWS, COLS))[None]
    beta = jnp.broadcast_to(beta, (ROWS, COLS))[None]
    here = d[...]
    control_next[...] = control[...] + alpha * here
    new = res[...] - alpha * image[...]
    res_next[...] = new
    d_next[...] = new + beta * here


VMEM = pl.BlockSpec(memory_space=pltpu.VMEM)
ANY = pl.BlockSpec(memory_space=pl.ANY)


def call(kernel, outs, scratch=(), given=VMEM, limit=LIMIT, flops=1000000):
    def shape_of(out):
        shape, dtype = out if isinstance(out[1], type) else (out, jnp.float32)
        return jax.ShapeDtypeStruct(shape, dtype)

    return lambda *arrays: pl.pallas_call(
        kernel,
        out_shape=tuple(shape_of(out) for out in outs),
        in_specs=[given] * len(arrays),
        out_specs=tuple([VMEM] * len(outs)),
        scratch_shapes=[pltpu.VMEM(s, jnp.float32) if isinstance(s, tuple) else s for s in scratch],
        compiler_params=pltpu.CompilerParams(vmem_limit_bytes=limit),
        cost_estimate=pl.CostEstimate(flops=flops, bytes_accessed=1000000, transcendentals=0),
    )(*arrays)


def step(x, axis, by):
    size = lax.axis_size(axis)
    return lax.ppermute(x, axis, [(i, (i + by) % size) for i in range(size)])


def exchange(x, axis):
    size = lax.axis_size(axis)
    blocks = x.reshape(size, x.shape[0] // size, COLS)
    return lax.all_to_all(blocks, axis, 0, 0, tiled=True).reshape(x.shape)


def local(
    control,
    residual,
    direction,
    land_mask,
    kappa_east,
    kappa_north,
    sigma,
    obs_weight,
    obs_cell,
    obs_owner,
    error_inverse,
):
    lats, lons, fields = lax.axis_size("lat"), lax.axis_size("lon"), lax.axis_size("obs")
    owners = lats * lons
    block = (LEV, ROWS, COLS)
    d = direction.reshape(block)
    res = residual.reshape(block)
    band, side, tables, own = call(
        pack_kernel,
        (
            (ROWS * (T_OWN + T_SIDE), COLS),
            (ROWS * T_SIDE, COLS),
            (4 * lats, COLS),
            (ROWS * T_OWN, COLS),
        ),
        (
            pltpu.VMEM((3 * ROWS, COLS), jnp.int32),
            (LEV, 1, SLOTS),
            (LEV, 1, LEV),
            (PADLEV, COLS),
            (COLS, COLS),
            pltpu.SemaphoreType.DMA((9,)),
        ),
        given=ANY,
        limit=56 * 1024 * 1024,
    )(
        direction.reshape(LEV * ROWS, COLS),
        land_mask,
        kappa_east,
        kappa_north,
        sigma.reshape(ROWS, COLS),
        jnp.transpose(obs_weight, (1, 0, 2)),
        obs_cell.reshape(2, COLS),
        obs_owner.reshape(2, COLS),
        jnp.transpose(error_inverse, (1, 0, 2)),
    )
    west = step(side, "lon", 1)
    tables = exchange(tables, "lat")
    band = pl.pallas_call(
        band_kernel,
        out_shape=jax.ShapeDtypeStruct(band.shape, jnp.float32),
        in_specs=[ANY, ANY],
        out_specs=ANY,
        scratch_shapes=[pltpu.SemaphoreType.DMA],
        input_output_aliases={0: 0},
        compiler_params=pltpu.CompilerParams(vmem_limit_bytes=LIMIT),
    )(band, west)
    south = step(band, "lat", 1)
    (tables,) = call(repeat_kernel, ((4 * owners, COLS),), flops=20000000000)(tables)
    tables = exchange(tables, "lon")
    part, aux, weights, marks = call(
        functools.partial(pick_kernel, lats, lons),
        (
            (PART_ROWS, COLS),
            (3, ROWS, COLS),
            (PADLEV, CANDIDATES),
            ((8, CANDIDATES), jnp.int32),
        ),
        ((2, T_FIELDS, ROWS, COLS), (PADLEV * ROWS, COLS)),
        flops=20000000000,
    )(own, west, south)
    parts = lax.all_gather(part, "obs", tiled=True)
    (source,) = call(
        functools.partial(spread_kernel, fields, owners),
        ((T_BACK + T_BACK_SIDE, ROWS, COLS),),
        (
            (PART_ROWS, COLS),
            (2 * PADLEV, owners),
            (2 * PADLEV, SLOTS),
            (PADLEV * ROWS, COLS),
        ),
    )(parts, tables, weights, marks, aux)
    north = step(source, "lat", -1)
    (side,) = call(back_kernel, ((2 * T_BACK_SIDE, ROWS, COLS),))(source, north)
    east = step(side, "lon", -1)
    image, sums = call(
        image_kernel, (block, (fields * lons, COLS)), ((2, T_BACK, ROWS, COLS),)
    )(source, north, east, d, res)
    sums = lax.all_to_all(sums, ("obs", "lon"), 0, 0, tiled=True)
    (sums,) = call(sum_kernel, ((lats, COLS),))(sums)
    sums = lax.all_to_all(sums, "lat", 0, 0, tiled=True)
    outs = call(step_kernel, (block, block, block))(sums, control.reshape(block), res, d, image)
    return tuple(out.reshape(direction.shape) for out in outs)


def solution(mesh):
    state = P("obs", None, "lat", "lon")
    placed = (
        state,
        state,
        state,
        P("lat", "lon"),
        P("lat", "lon"),
        P("lat", "lon"),
        P("obs", "lat", "lon"),
        P("obs", None, ("lat", "lon")),
        P(("lat", "lon")),
        P(("lat", "lon"), None),
        P(("lat", "lon"), None, None),
    )
    return jax.shard_map(
        local, mesh=mesh, in_specs=placed, out_specs=(state, state, state), check_vma=False
    )
```
